256 devices in a mesh: blk: 32 (over x, z), kv: 8 (over y, core).
Axes of the slice: x: 4, y: 4, z: 8, core: 2. Of those that a mesh axis runs over, the one named last changes fastest.
Arguments:
- context: bfloat16 [16384, 4096], P('blk'), may hold values from -6 to 6
- question: bfloat16 [256, 4096], P('blk'), may hold values from -6 to 6
- norm_gain: float32 [4096], replicated, may hold values from 0.1 to 1.9
- w_query: bfloat16 [4096, 4096], P(None, 'kv')
- w_key: bfloat16 [4096, 1024], P(None, 'kv'), as said below
- w_value: bfloat16 [4096, 1024], P(None, 'kv'), may hold values from -0.09375 to 0.09375
- w_out: bfloat16 [4096, 4096], P('kv'), may hold values from -0.375 to 0.375
- block_len: int32 [32], replicated, may hold values from 1 to 512, as said below
- question_len: int32 [1], replicated, may hold values from 64 to 256
Outputs:
- context_out: bfloat16 [16384, 4096], P('blk', 'kv')
- question_out: bfloat16 [256, 4096], P('blk', 'kv')
The draws below stay inside these ranges and needn't reach their ends.
Inputs may be any that keep to these rules, and one draw needn't show every extreme that they name: `block_len`: every block holds 512 live tokens except the last, which holds 1 to 511. `w_key`: entries are those of a fan-in scaled projection.
All inputs are finite; a program needn't handle non-finite values.
Results may differ from the reference program's by a relative error of at most 0.022.
Values may be sent and summed in bfloat16 or wider, within the bound.
No kernel may reach another device: no remote copies, remote signals or barrier semaphores. Data moves between devices by JAX's collectives and lax.ppermute only.
A program may use at most 128 MiB of HBM per device.

```python
import jax
import jax.numpy as jnp
from jax import lax

D = 4096
HQ = 32
KVH = 8
HD = 128
BLK = 512
QN = 256
CTX = 16384
N_BLK = 32
N_KV = 8


def shared_matrix(key):
    return jnp.clip(jax.random.normal(jax.random.fold_in(key, 91), (D, KVH * HD), jnp.float32), -6.0, 6.0)


def draw_w_key(key, part):
    shared = shared_matrix(key)
    return (shared * D ** (-0.5)).astype(jnp.bfloat16)


def draw_w_query(key, part):
    key = jax.random.fold_in(key, 3)
    random_part = jnp.clip(jax.random.normal(key, (D, HQ * HD), jnp.float32), -6.0, 6.0) * (2.0 * D ** (-0.5))
    values = random_part
    return values.astype(jnp.bfloat16)


def draw_block_len(key, part):
    key = jax.random.fold_in(key, 7)
    last_len = jax.random.randint(key, (1,), 1, BLK, jnp.int32)
    return jnp.concatenate([jnp.full((N_BLK - 1,), BLK, jnp.int32), last_len])


def block_scale(key, shape, split, low, top_value):
    factor_of, own = 1.0, jax.random.fold_in(key, 6)
    for axis_at, blocks in split:
        heights = jnp.exp(jax.random.uniform(jax.random.fold_in(own, axis_at), (blocks,), jnp.float32, low / len(split), top_value / len(split)))
        factor_of = factor_of * jnp.repeat(heights, shape[axis_at] // blocks).reshape([-1 if axis == axis_at else 1 for axis in range(len(shape))])
    return factor_of


def bell_draw(key, dims, scale, bound, shards=(), kind=jnp.bfloat16):
    gain = block_scale(key, dims, shards, -0.22, 0.18) if shards else 1.0
    entries = jax.random.normal(key, dims, jnp.float32) * scale * gain
    return jnp.minimum(jnp.maximum(entries, -bound), bound).astype(kind)


def setup_inputs(seed: int = 0) -> dict:
    arg_keys = jax.random.split(jax.random.key(seed), 10)
    return {
        "context": bell_draw(arg_keys[0], (CTX, D), 1.0, 6.0, ((0, 32),)),
        "question": bell_draw(arg_keys[1], (QN, D), 1.0, 6.0, ((0, 32),)),
        "norm_gain": jnp.clip(1.0 + 0.18 * jax.random.normal(arg_keys[2], (D,), jnp.float32), 0.1, 1.9),
        "w_query": draw_w_query(jax.random.fold_in(arg_keys[9], 71), 0),
        "w_key": draw_w_key(jax.random.fold_in(arg_keys[9], 71), 0),
        "w_value": bell_draw(arg_keys[5], (D, KVH * HD), D ** -0.5, 0.09375, ((1, 8),)),
        "w_out": bell_draw(arg_keys[6], (HQ * HD, D), (HQ * HD // 16) ** -0.5, 0.375, ((0, 8),)),
        "block_len": draw_block_len(jax.random.fold_in(arg_keys[9], 71), 0),
        "question_len": jax.random.randint(arg_keys[8], (1,), QN // 4, QN + 1).astype(jnp.int32),
    }


epsilon = 1e-05
rope_base = 500000.0
masked_score = -1e+30

def normalize(rows_in, gain_full):
    values = rows_in.astype(jnp.float32)
    factor = lax.rsqrt(lax.optimization_barrier(jnp.mean(values * values, axis=-1, keepdims=True)) + epsilon)
    return (values * factor * gain_full).astype(jnp.bfloat16)

def rotate(heads_in, positions):
    head_width = heads_in.shape[-1]
    half_width = head_width // 2
    inverse_freq = rope_base ** (-2.0 * jnp.arange(half_width, dtype=jnp.float32) / head_width)
    angles = positions.astype(jnp.float32)[:, None] * inverse_freq[None, :]
    cosine = jnp.cos(angles)[:, None, :]
    sine_part = jnp.sin(angles)[:, None, :]
    former = heads_in[..., :half_width]
    latter = heads_in[..., half_width:]
    return jnp.concatenate([former * cosine - latter * sine_part, latter * cosine + former * sine_part], axis=-1)

def project(normed, weight, positions):
    product = jnp.dot(normed, weight, preferred_element_type=jnp.float32)
    row_count = product.shape[0]
    heads_in = product.reshape(row_count, -1, HD)
    if positions is not None:
        heads_in = rotate(heads_in, positions)
    return heads_in.reshape(row_count, -1).astype(jnp.bfloat16)

def attend(queries, key_rows, value_rows, allowed, row_valid, kv_heads):
    row_count = queries.shape[0]
    key_count = key_rows.shape[0]
    shaped_query = queries.astype(jnp.float32).reshape(row_count, kv_heads, -1, HD)
    shaped_key = key_rows.astype(jnp.float32).reshape(key_count, kv_heads, HD)
    shaped_value = value_rows.astype(jnp.float32).reshape(key_count, kv_heads, HD)
    scores = jnp.einsum('rkgh,skh->kgrs', shaped_query, shaped_key) * HD ** (-0.5)
    masked = jnp.where(allowed, scores, masked_score)
    highest = lax.optimization_barrier(jnp.max(masked, axis=-1, keepdims=True))
    weights = jnp.where(allowed, jnp.exp(masked - highest), 0.0)
    totals = lax.optimization_barrier(jnp.sum(weights, axis=-1))
    rounded = lax.optimization_barrier(weights.astype(jnp.bfloat16)).astype(jnp.float32)
    mixture = jnp.einsum('kgrs,skh->rkgh', rounded, shaped_value)
    result = mixture / jnp.transpose(totals, (2, 0, 1))[..., None]
    result = jnp.where(row_valid[:, None, None, None], result, 0.0)
    return result.reshape(row_count, -1).astype(jnp.bfloat16)

def reference(context, question, norm_gain, w_query, w_key, w_value, w_out, block_len, question_len):
    group_size = HQ // KVH
    total_ctx = jnp.sum(block_len)
    live_questions = question_len[0]
    ctx_normed = normalize(context, norm_gain)
    que_normed = normalize(question, norm_gain)
    ctx_positions = jnp.arange(CTX, dtype=jnp.int32)
    que_positions = total_ctx + jnp.arange(QN, dtype=jnp.int32)
    ctx_query = project(ctx_normed, w_query, ctx_positions)
    ctx_key = project(ctx_normed, w_key, ctx_positions)
    ctx_value = project(ctx_normed, w_value, None)
    que_query = project(que_normed, w_query, que_positions)
    que_key = project(que_normed, w_key, que_positions)
    que_value = project(que_normed, w_value, None)
    token_ids = jnp.arange(BLK, dtype=jnp.int32)
    anchor_key = ctx_key[:BLK]
    anchor_value = ctx_value[:BLK]

    def block_attention(block_id):
        first_row = block_id * BLK
        queries = lax.dynamic_slice_in_dim(ctx_query, first_row, BLK, 0)
        own_key = lax.dynamic_slice_in_dim(ctx_key, first_row, BLK, 0)
        own_value = lax.dynamic_slice_in_dim(ctx_value, first_row, BLK, 0)
        key_rows = jnp.concatenate([anchor_key, own_key], 0)
        value_rows = jnp.concatenate([anchor_value, own_value], 0)
        allowed = jnp.concatenate([jnp.broadcast_to(block_id > 0, (BLK, BLK)), token_ids[None, :] <= token_ids[:, None]], 1)
        row_valid = token_ids < block_len[block_id]
        return attend(queries, key_rows, value_rows, allowed, row_valid, KVH)
    ctx_attn = lax.map(block_attention, jnp.arange(N_BLK, dtype=jnp.int32)).reshape(CTX, HQ * HD)
    all_key = jnp.concatenate([ctx_key, que_key], 0)
    all_value = jnp.concatenate([ctx_value, que_value], 0)
    ctx_ids = jnp.arange(CTX, dtype=jnp.int32)
    ctx_live = ctx_ids % BLK < block_len[ctx_ids // BLK]
    que_ids = jnp.arange(QN, dtype=jnp.int32)
    que_allowed = jnp.concatenate([jnp.broadcast_to(ctx_live[None, :], (QN, CTX)), que_ids[None, :] <= que_ids[:, None]], 1)
    que_valid = que_ids < live_questions

    def question_attention(group_id):
        queries = lax.dynamic_slice_in_dim(que_query, group_id * group_size * HD, group_size * HD, 1)
        key_rows = lax.dynamic_slice_in_dim(all_key, group_id * HD, HD, 1)
        value_rows = lax.dynamic_slice_in_dim(all_value, group_id * HD, HD, 1)
        return attend(queries, key_rows, value_rows, que_allowed, que_valid, 1)
    que_attn = jnp.transpose(lax.map(question_attention, jnp.arange(KVH, dtype=jnp.int32)), (1, 0, 2)).reshape(QN, HQ * HD)
    attended = jnp.concatenate([ctx_attn, que_attn], 0)
    group_cols = HQ * HD // N_KV
    summed = jnp.zeros((CTX + QN, D), jnp.float32)
    for group_id in range(N_KV):
        product = jnp.dot(attended[:, group_id * group_cols:(group_id + 1) * group_cols], w_out[group_id * group_cols:(group_id + 1) * group_cols], preferred_element_type=jnp.float32)
        summed = summed + lax.optimization_barrier(product.astype(jnp.bfloat16)).astype(jnp.float32)
    projected = summed.astype(jnp.bfloat16)
    return (projected[:CTX], projected[CTX:])
```

```python
import functools

import jax
import jax.numpy as jnp
import numpy as np
from jax import lax
from jax.experimental import pallas as pl
from jax.experimental.pallas import tpu as pltpu
from jax.sharding import PartitionSpec as P

HD = 128
HEADS = 4
BLK = 512
QROWS = 8
NX, NZ, NY, NC = 4, 8, 4, 2
N_BLK, N_KV = NX * NZ, NY * NC
QN = N_BLK * QROWS
D = 4096
FEAT = D // N_KV
KC = 512
ROWS = 256

epsilon = 1e-05
rope_base = 500000.0
masked_score = -1e30
q_scale = float(HD**-0.5 * np.log2(np.e))
log2_e = float(np.log2(np.e))

bf16 = jnp.bfloat16
f32 = jnp.float32


def angle_tables(positions):
    inverse_freq = rope_base ** (-2.0 * np.arange(HD // 2, dtype=np.float64) / HD)
    angles = np.asarray(positions, np.float64)[:, None] * inverse_freq[None, :]
    angles = np.concatenate([angles, angles], 1)
    return np.cos(angles).astype(np.float32), np.sin(angles).astype(np.float32)


def params(semantics=1, limit=40):
    return pltpu.CompilerParams(
        dimension_semantics=("arbitrary",) * semantics, vmem_limit_bytes=limit * 2**20
    )


def cost(flops, bytes_accessed, transcendentals=0):
    return pl.CostEstimate(
        flops=flops, bytes_accessed=bytes_accessed, transcendentals=transcendentals
    )


def add_angles(first, second):
    return (
        first[0] * second[0] - first[1] * second[1],
        first[1] * second[0] + first[0] * second[1],
    )


def rotated(head, cosine, sine_signed):
    return head * cosine + pltpu.roll(head, HD // 2, 1) * sine_signed


def signed(sine):
    lane = lax.broadcasted_iota(jnp.int32, sine.shape, 1)
    return jnp.where(lane < HD // 2, -sine, sine)


def dot(a, b):
    return jnp.dot(a, b, preferred_element_type=f32)


def dot_t(a, b):
    return lax.dot_general(a, b, (((1,), (1,)), ((), ())), preferred_element_type=f32)


def lane_folded(values):
    total = values[:, :HD]
    for part in range(1, values.shape[1] // HD):
        total = total + values[:, part * HD : (part + 1) * HD]
    return total


def squares_to_factor(squares):
    mean = jnp.sum(squares, axis=-1, keepdims=True) * (1.0 / D)
    return lax.rsqrt(mean + epsilon)


def question_kernel(
    len_ref, where_ref, x_ref, gain_ref, wq_ref, wk_ref, wv_ref, ct_ref, st_ref, cb_ref, sb_ref,
    q_ref, kv_ref, acc_ref, sq_ref,
):
    step = pl.program_id(0)

    @pl.when(step == 0)
    def _():
        acc_ref[...] = jnp.zeros_like(acc_ref)
        sq_ref[...] = jnp.zeros_like(sq_ref)

    x = x_ref[...].astype(f32)
    sq_ref[...] += lane_folded(x * x)
    scaled = (x * gain_ref[...]).astype(bf16)
    acc_ref[:, : HEADS * HD] += dot(scaled, wq_ref[...])
    acc_ref[:, HEADS * HD : (HEADS + 1) * HD] += dot(scaled, wk_ref[...])
    acc_ref[:, (HEADS + 1) * HD :] += dot(scaled, wv_ref[...])

    @pl.when(step == pl.num_programs(0) - 1)
    def _():
        factor = squares_to_factor(sq_ref[...])
        total = len_ref[0]
        for b in range(1, N_BLK):
            total = total + len_ref[b]
        high, low = total // BLK, lax.rem(total, BLK)
        base = add_angles(
            (cb_ref[pl.ds(high, 1), :], sb_ref[pl.ds(high, 1), :]),
            (ct_ref[pl.ds(low, 1), :], st_ref[pl.ds(low, 1), :]),
        )
        rows = pl.ds(pl.multiple_of(where_ref[0] * QROWS, QROWS), QROWS)
        cosine, sine = add_angles((ct_ref[rows, :], st_ref[rows, :]), base)
        sine = signed(sine)
        for h in range(HEADS + 1):
            head = acc_ref[:, h * HD : (h + 1) * HD] * factor
            head = rotated(head, cosine, sine)
            if h < HEADS:
                q_ref[:, h * HD : (h + 1) * HD] = (head * q_scale).astype(bf16)
            else:
                kv_ref[:, :HD] = head.astype(bf16)
        kv_ref[:, HD:] = (acc_ref[:, (HEADS + 1) * HD :] * factor).astype(bf16)


def whole(shape):
    return pl.BlockSpec(shape, lambda *_: (0,) * len(shape))


smem = pl.BlockSpec(memory_space=pltpu.SMEM)


def question_projection(block_len, where, question, gain, wq, wk, wv, tables):
    return pl.pallas_call(
        question_kernel,
        grid=(D // KC,),
        in_specs=[
            smem,
            smem,
            pl.BlockSpec((QROWS, KC), lambda k: (0, k)),
            pl.BlockSpec((1, KC), lambda k: (0, k)),
            pl.BlockSpec((KC, HEADS * HD), lambda k: (k, 0)),
            pl.BlockSpec((KC, HD), lambda k: (k, 0)),
            pl.BlockSpec((KC, HD), lambda k: (k, 0)),
            whole((BLK, HD)),
            whole((BLK, HD)),
            whole((N_BLK + 1, HD)),
            whole((N_BLK + 1, HD)),
        ],
        out_specs=[whole((QROWS, HEADS * HD)), whole((QROWS, 2 * HD))],
        out_shape=[
            jax.ShapeDtypeStruct((QROWS, HEADS * HD), bf16),
            jax.ShapeDtypeStruct((QROWS, 2 * HD), bf16),
        ],
        scratch_shapes=[
            pltpu.VMEM((QROWS, (HEADS + 2) * HD), f32),
            pltpu.VMEM((QROWS, HD), f32),
        ],
        compiler_params=params(),
        cost_estimate=cost(2 * QROWS * D * 768 * 32, D * 768 * 2),
        name="question_projection",
    )(block_len, where, question, gain, wq, wk, wv, *tables)


def kv_kernel(
    where_ref, x_ref, gain_ref, wk_ref, wv_ref, ct_ref, st_ref, cb_ref, sb_ref,
    kv_ref, factor_ref, acc_ref, sq_ref,
):
    step = pl.program_id(0)

    @pl.when(step == 0)
    def _():
        acc_ref[...] = jnp.zeros_like(acc_ref)
        sq_ref[...] = jnp.zeros_like(sq_ref)

    x = x_ref[...].astype(f32)
    sq_ref[...] += lane_folded(x * x)
    scaled = (x * gain_ref[...]).astype(bf16)
    weights = jnp.concatenate([wk_ref[...], wv_ref[...]], axis=1)
    acc_ref[...] += dot(scaled, weights)

    @pl.when(step == pl.num_programs(0) - 1)
    def _():
        factor = squares_to_factor(sq_ref[...])
        block = pl.ds(where_ref[0], 1)
        cosine, sine = add_angles(
            (ct_ref[...], st_ref[...]), (cb_ref[block, :], sb_ref[block, :])
        )
        head = rotated(acc_ref[:, :HD] * factor, cosine, signed(sine))
        kv_ref[:, :HD] = head.astype(bf16)
        kv_ref[:, HD:] = (acc_ref[:, HD:] * factor).astype(bf16)
        factor_ref[...] = jnp.broadcast_to(factor, factor_ref.shape)


def kv_projection(where, context, gain, wk, wv, tables):
    return pl.pallas_call(
        kv_kernel,
        grid=(D // KC,),
        in_specs=[
            smem,
            pl.BlockSpec((BLK, KC), lambda k: (0, k)),
            pl.BlockSpec((1, KC), lambda k: (0, k)),
            pl.BlockSpec((KC, HD), lambda k: (k, 0)),
            pl.BlockSpec((KC, HD), lambda k: (k, 0)),
            whole((BLK, HD)),
            whole((BLK, HD)),
            whole((N_BLK + 1, HD)),
            whole((N_BLK + 1, HD)),
        ],
        out_specs=[whole((BLK, 2 * HD)), whole((BLK, HD))],
        out_shape=[
            jax.ShapeDtypeStruct((BLK, 2 * HD), bf16),
            jax.ShapeDtypeStruct((BLK, HD), f32),
        ],
        scratch_shapes=[pltpu.VMEM((BLK, 2 * HD), f32), pltpu.VMEM((BLK, HD), f32)],
        compiler_params=params(),
        cost_estimate=cost(2 * BLK * D * 256 * 3, D * 256 * 2 + BLK * D * 2),
        name="kv_projection",
    )(where, context, gain, wk, wv, *tables)


def query_kernel(
    where_ref, x_ref, gain_ref, wq_ref, factor_ref, ct_ref, st_ref, cb_ref, sb_ref,
    q_ref, acc_ref,
):
    step = pl.program_id(0)

    @pl.when(step == 0)
    def _():
        acc_ref[...] = jnp.zeros_like(acc_ref)

    scaled = (x_ref[...].astype(f32) * gain_ref[...]).astype(bf16)
    acc_ref[...] += dot(scaled, wq_ref[...])

    @pl.when(step == pl.num_programs(0) - 1)
    def _():
        block = pl.ds(where_ref[0], 1)
        cosine, sine = add_angles(
            (ct_ref[...], st_ref[...]), (cb_ref[block, :], sb_ref[block, :])
        )
        scale = factor_ref[...] * q_scale
        cosine, sine = cosine * scale, signed(sine) * scale
        for h in range(HEADS):
            head = acc_ref[:, h * HD : (h + 1) * HD]
            q_ref[h] = rotated(head, cosine, sine).astype(bf16)


def query_projection(where, context, gain, wq, factor, tables):
    return pl.pallas_call(
        query_kernel,
        grid=(D // KC,),
        in_specs=[
            smem,
            pl.BlockSpec((BLK, KC), lambda k: (0, k)),
            pl.BlockSpec((1, KC), lambda k: (0, k)),
            pl.BlockSpec((KC, HEADS * HD), lambda k: (k, 0)),
            whole((BLK, HD)),
            whole((BLK, HD)),
            whole((BLK, HD)),
            whole((N_BLK + 1, HD)),
            whole((N_BLK + 1, HD)),
        ],
        out_specs=whole((HEADS, BLK, HD)),
        out_shape=jax.ShapeDtypeStruct((HEADS, BLK, HD), bf16),
        scratch_shapes=[pltpu.VMEM((BLK, HEADS * HD), f32)],
        compiler_params=params(),
        cost_estimate=cost(2 * BLK * D * 512, D * 512 * 2 + BLK * D * 2),
        name="query_projection",
    )(where, context, gain, wq, factor, *tables)


def with_ones(values):
    return jnp.concatenate([values, jnp.ones_like(values)], axis=1)


def own_kernel(q_ref, kv_ref, o_ref, lse_ref):
    row = lax.broadcasted_iota(jnp.int32, (ROWS, ROWS), 0)
    column = lax.broadcasted_iota(jnp.int32, (ROWS, ROWS), 1)
    causal = column <= row
    for h in range(HEADS):
        for r in range(BLK // ROWS):
            rows = slice(r * ROWS, (r + 1) * ROWS)
            q = q_ref[h, rows, :]
            diagonal = dot_t(q, kv_ref[rows, :HD])
            diagonal = jnp.where(causal, diagonal, masked_score)
            highest = jnp.max(diagonal, axis=-1, keepdims=True)
            if r:
                earlier = dot_t(q, kv_ref[: r * ROWS, :HD])
                highest = jnp.maximum(highest, jnp.max(earlier, axis=-1, keepdims=True))
            weights = jnp.exp2(diagonal - highest).astype(bf16)
            mixture = dot(weights, with_ones(kv_ref[rows, HD:]))
            if r:
                weights = jnp.exp2(earlier - highest).astype(bf16)
                mixture = mixture + dot(weights, with_ones(kv_ref[: r * ROWS, HD:]))
            totals = mixture[:, HD:]
            o_ref[h, rows, :] = mixture[:, :HD] / totals
            lse_ref[h, rows, :] = highest + jnp.log(totals) * log2_e


def own_attention(q, kv):
    return pl.pallas_call(
        own_kernel,
        out_shape=[jax.ShapeDtypeStruct((HEADS, BLK, HD), f32)] * 2,
        in_specs=[pl.BlockSpec(memory_space=pltpu.VMEM)] * 2,
        out_specs=[pl.BlockSpec(memory_space=pltpu.VMEM)] * 2,
        compiler_params=pltpu.CompilerParams(vmem_limit_bytes=40 * 2**20),
        cost_estimate=cost(HEADS * BLK * BLK * HD * 8, 3 * 2**20, HEADS * BLK * BLK),
        name="own_attention",
    )(q, kv)


def gathered_source(group, x_at, z_at):
    dx = group % 4
    dz = (group // 4) % 4
    dz = jnp.where(dz == 3, -1, dz) + 4 * (group // 16)
    return ((x_at - dx + NX) % NX) * NZ + (z_at - dz + 2 * NZ) % NZ


def question_attention_kernel(len_ref, where_ref, qa_ref, qb_ref, kv_ref, own_ref, out_ref, buf_ref):
    blk_at = where_ref[0]
    x_at, z_at = blk_at // NZ, lax.rem(blk_at, NZ)
    live = lax.broadcasted_iota(jnp.int32, (QN, BLK), 1) < len_ref[blk_at]
    group = lax.broadcasted_iota(jnp.int32, (QN, HD), 0)
    question_id = gathered_source(group // QROWS, x_at, z_at) * QROWS + group % QROWS
    key_id = lax.broadcasted_iota(jnp.int32, (QN, HD), 1)
    seen = (key_id < QROWS) & (key_id + blk_at * QROWS <= question_id)
    own = jnp.concatenate([own_ref[...].astype(f32), jnp.zeros((HD - QROWS, 2 * HD), f32)], 0)
    own = own.astype(bf16)
    values = with_ones(kv_ref[:, HD:])
    own_values = with_ones(own[:, HD:])
    lane = key_id
    tile = jnp.zeros((QN, HD), f32)
    for h in range(HEADS):
        cols = slice(h * HD, (h + 1) * HD)
        q = jnp.concatenate([qa_ref[:, cols], qb_ref[:, cols]], axis=0)
        scores = jnp.where(live, dot_t(q, kv_ref[:, :HD]), masked_score)
        own_scores = jnp.where(seen, dot_t(q, own[:, :HD]), masked_score)
        highest = jnp.maximum(
            jnp.max(scores, axis=-1, keepdims=True), jnp.max(own_scores, axis=-1, keepdims=True)
        )
        mixture = dot(jnp.exp2(scores - highest).astype(bf16), values)
        mixture = mixture + dot(jnp.exp2(own_scores - highest).astype(bf16), own_values)
        totals = mixture[:, HD:]
        buf_ref[:, cols] = mixture[:, :HD] / totals
        lse = highest + jnp.log(totals) * log2_e
        tile = jnp.where(lane // 32 == h, lse, tile)
    high = tile.astype(bf16).astype(f32)
    rest = tile - high
    middle = rest.astype(bf16).astype(f32)
    piece = lane % 32
    buf_ref[:, HEADS * HD :] = jnp.where(
        piece == 0, high, jnp.where(piece == 1, middle, jnp.where(piece == 2, rest - middle, 0.0))
    )
    for g in range(N_BLK):
        source = gathered_source(jnp.int32(g), x_at, z_at)
        out_ref[source] = buf_ref[g * QROWS : (g + 1) * QROWS, :].astype(bf16)


def question_attention(block_len, where, first_half, second_half, kv, own):
    width = (HEADS + 1) * HD
    vmem = pl.BlockSpec(memory_space=pltpu.VMEM)
    return pl.pallas_call(
        question_attention_kernel,
        out_shape=jax.ShapeDtypeStruct((N_BLK, QROWS, width), bf16),
        in_specs=[smem, smem, vmem, vmem, vmem, vmem],
        out_specs=vmem,
        scratch_shapes=[pltpu.VMEM((QN, width), f32)],
        compiler_params=pltpu.CompilerParams(vmem_limit_bytes=40 * 2**20),
        cost_estimate=cost(HEADS * QN * 640 * HD * 8, 2**20, HEADS * QN * 640),
        name="question_attention",
    )(block_len, where, first_half, second_half, kv, own)


def context_kernel(
    len_ref, where_ref, q_ref, o_ref, lse_ref, a0_ref, a1_ref, a2_ref, a3_ref, w_hbm,
    keep_ref, send_ref, w_ref, akv_ref, att_ref, sem,
):
    step = pl.program_id(0)
    blk_at, kv_at = where_ref[0], where_ref[1]
    y_at, c_at = kv_at // NC, lax.rem(kv_at, NC)
    copy = pltpu.make_async_copy(w_hbm, w_ref, sem)

    @pl.when(step == 0)
    def _():
        copy.start()
        x_at = blk_at // NZ
        for x, ref in enumerate((a0_ref, a1_ref, a2_ref, a3_ref)):

            @pl.when(x_at == x)
            def _(ref=ref):
                akv_ref[...] = ref[...]

    first = blk_at == 0
    row = lax.broadcasted_iota(jnp.int32, (ROWS, HD), 0) + step * ROWS
    valid = row < len_ref[blk_at]
    values = with_ones(akv_ref[:, HD:])
    for h in range(HEADS):
        scores = dot_t(q_ref[h], akv_ref[:, :HD])
        highest = jnp.max(scores, axis=-1, keepdims=True)
        mixture = dot(jnp.exp2(scores - highest).astype(bf16), values)
        own_lse = lse_ref[h]
        top = jnp.where(first, own_lse, jnp.maximum(own_lse, highest))
        own_part = jnp.exp2(own_lse - top)
        anchor_part = jnp.where(first, 0.0, jnp.exp2(jnp.minimum(highest - top, 0.0)))
        result = (o_ref[h] * own_part + mixture[:, :HD] * anchor_part) / (
            own_part + mixture[:, HD:] * anchor_part
        )
        att_ref[:, h * HD : (h + 1) * HD] = jnp.where(valid, result, 0.0).astype(bf16)

    @pl.when(step == 0)
    def _():
        copy.wait()

    for d in range(NY):
        to_y = lax.rem(y_at + d, NY)
        for out, to_c in ((send_ref, 1 - c_at), (keep_ref, c_at)):
            column = pl.multiple_of((to_y * NC + to_c) * FEAT, FEAT)
            out[d] = dot(att_ref[...], w_ref[:, pl.ds(column, FEAT)]).astype(bf16)


def context_attention(block_len, where, q, own_o, own_lse, anchors, w_out):
    part = pl.BlockSpec((HEADS, ROWS, HD), lambda r: (0, r, 0))
    out = pl.BlockSpec((NY, ROWS, FEAT), lambda r: (0, r, 0))
    return pl.pallas_call(
        context_kernel,
        grid=(BLK // ROWS,),
        in_specs=[smem, smem, part, part, part]
        + [whole((BLK, 2 * HD))] * 4
        + [pl.BlockSpec(memory_space=pl.ANY)],
        out_specs=[out, out],
        out_shape=[jax.ShapeDtypeStruct((NY, BLK, FEAT), bf16)] * 2,
        scratch_shapes=[
            pltpu.VMEM((HEADS * HD, D), bf16),
            pltpu.VMEM((BLK, 2 * HD), bf16),
            pltpu.VMEM((ROWS, HEADS * HD), bf16),
            pltpu.SemaphoreType.DMA,
        ],
        compiler_params=params(),
        cost_estimate=cost(2 * BLK * 512 * D + HEADS * BLK * BLK * HD * 8, 12 * 2**20, HEADS * BLK * BLK),
        name="context_attention",
    )(block_len, where, q, own_o, own_lse, *anchors, w_out)


def merge_kernel(qlen_ref, where_ref, parts_ref, w_ref, out_ref, att_ref):
    @pl.when(pl.program_id(0) == 0)
    def _():
        parts = parts_ref[...].astype(f32)
        row = lax.broadcasted_iota(jnp.int32, (QROWS, HD), 0) + where_ref[0] * QROWS
        valid = row < qlen_ref[0]
        stats = parts[:, :, HEADS * HD :]
        for h in range(HEADS):
            at = h * 32
            lse = (stats[:, :, at : at + 1] + stats[:, :, at + 1 : at + 2]) + stats[:, :, at + 2 : at + 3]
            top = jnp.max(lse, axis=0, keepdims=True)
            share = jnp.exp2(lse - top)
            mixture = jnp.sum(parts[:, :, h * HD : (h + 1) * HD] * share, axis=0)
            result = mixture / jnp.sum(share, axis=0)
            att_ref[:, h * HD : (h + 1) * HD] = jnp.where(valid, result, 0.0)

    out_ref[0] = dot(att_ref[...].astype(bf16), w_ref[...]).astype(bf16)


def merge_and_project(question_len, where, parts, w_out):
    return pl.pallas_call(
        merge_kernel,
        grid=(N_KV,),
        in_specs=[
            smem,
            smem,
            whole(parts.shape),
            pl.BlockSpec((HEADS * HD, FEAT), lambda k: (0, k)),
        ],
        out_specs=pl.BlockSpec((1, QROWS, FEAT), lambda k: (k, 0, 0)),
        out_shape=jax.ShapeDtypeStruct((N_KV, QROWS, FEAT), bf16),
        scratch_shapes=[pltpu.VMEM((QROWS, HEADS * HD), f32)],
        compiler_params=params(),
        cost_estimate=cost(2 * QROWS * 512 * D * 32, 5 * 2**20),
        name="merge_and_project",
    )(question_len, where, parts, w_out)


def shift_x(value, by):
    pairs = [(x * NZ + z, (x + by) % NX * NZ + z) for x in range(NX) for z in range(NZ)]
    return lax.ppermute(value, "blk", pairs)


def shift_z(value, by):
    pairs = [(x * NZ + z, x * NZ + (z + by) % NZ) for x in range(NX) for z in range(NZ)]
    return lax.ppermute(value, "blk", pairs)


def shift_y(value, by):
    pairs = [(y * NC + c, (y + by) % NY * NC + c) for y in range(NY) for c in range(NC)]
    return lax.ppermute(value, "kv", pairs)


def swap_cores(value):
    pairs = [(y * NC + c, y * NC + 1 - c) for y in range(NY) for c in range(NC)]
    return lax.ppermute(value, "kv", pairs)


def gather_questions(queries):
    rows = jnp.concatenate([queries] + [shift_x(queries, k) for k in (1, 2, 3)], 0)
    rows = jnp.concatenate([rows] + [shift_z(rows, k) for k in (1, 2, -1)], 0)
    return rows, shift_z(rows, 4)


def anchors_of(kv, blk_at):
    z_at = blk_at % NZ
    first = jnp.where(blk_at == 0, kv, jnp.zeros_like(kv))
    held = first + lax.ppermute(kv, "blk", [(0, 3)]) + lax.ppermute(kv, "blk", [(0, 5)])
    held = (
        held
        + lax.ppermute(held, "blk", [(0, 1), (3, 4), (5, 6)])
        + lax.ppermute(held, "blk", [(0, 7), (3, 2)])
    )
    others = [
        lax.ppermute(held, "blk", [(z, x * NZ + z) for z in range(NZ)]) for x in range(1, NX)
    ]
    return [held] + others


def body(context, question, norm_gain, w_query, w_key, w_value, w_out, block_len, question_len):
    blk_at = lax.axis_index("blk").astype(jnp.int32)
    kv_at = lax.axis_index("kv").astype(jnp.int32)
    where = jnp.stack([blk_at, kv_at])
    tables = [jnp.asarray(t) for t in angle_tables(np.arange(BLK))]
    tables += [jnp.asarray(t) for t in angle_tables(np.arange(N_BLK + 1) * BLK)]
    gain = norm_gain.reshape(1, D)

    own_q, own_kv = question_projection(
        block_len, where, question, gain, w_query, w_key, w_value, tables
    )
    first_half, second_half = gather_questions(own_q)
    kv, factor = kv_projection(where, context, gain, w_key, w_value, tables)
    anchors = anchors_of(kv, blk_at)
    q = query_projection(where, context, gain, w_query, factor, tables)
    own_o, own_lse = own_attention(q, kv)
    parts = question_attention(block_len, where, first_half, second_half, kv, own_kv)

    keep, send = context_attention(block_len, where, q, own_o, own_lse, anchors, w_out)
    got = swap_cores(send)

    def both(d):
        return (keep[d].astype(f32) + got[d].astype(f32)).astype(bf16)

    arrived = [shift_y(both(d), d) for d in (1, 3, 2)]
    context_out = keep[0].astype(f32) + got[0].astype(f32)
    for part in arrived:
        context_out = context_out + part.astype(f32)

    parts = lax.all_to_all(parts, "blk", 0, 0)
    question_part = merge_and_project(question_len, where, parts, w_out)
    question_part = lax.all_to_all(question_part, "kv", 0, 0)
    question_out = jnp.sum(question_part.astype(f32), axis=0)
    return context_out.astype(bf16), question_out.astype(bf16)


def solution(mesh):
    return jax.shard_map(
        body,
        mesh=mesh,
        in_specs=(
            P("blk", None),
            P("blk", None),
            P(),
            P(None, "kv"),
            P(None, "kv"),
            P(None, "kv"),
            P("kv", None),
            P(),
            P(),
        ),
        out_specs=(P("blk", "kv"), P("blk", "kv")),
        check_vma=False,
    )
```

```python
import functools

import jax
import jax.numpy as jnp
import numpy as np
from jax import lax
from jax.experimental import pallas as pl
from jax.experimental.pallas import tpu as pltpu
from jax.sharding import PartitionSpec as P

HD = 128
HEADS = 4
BLK = 512
QROWS = 8
NX, NZ, NY, NC = 4, 8, 4, 2
N_BLK, N_KV = NX * NZ, NY * NC
QN = N_BLK * QROWS
D = 4096
FEAT = D // N_KV
KC = 512
ROWS = 256
QPAD = 16
ALL_ROWS = BLK + QPAD
FIRST = 272

epsilon = 1e-05
rope_base = 500000.0
masked_score = -1e30
q_scale = float(HD**-0.5 * np.log2(np.e))
log2_e = float(np.log2(np.e))

bf16 = jnp.bfloat16
f32 = jnp.float32


def angle_tables(positions):
    inverse_freq = rope_base ** (-2.0 * np.arange(HD // 2, dtype=np.float64) / HD)
    angles = np.asarray(positions, np.float64)[:, None] * inverse_freq[None, :]
    angles = np.concatenate([angles, angles], 1)
    return np.cos(angles).astype(np.float32), np.sin(angles).astype(np.float32)


def params(limit=24):
    return pltpu.CompilerParams(vmem_limit_bytes=limit * 2**20)


def cost(flops, bytes_accessed, transcendentals=0):
    return pl.CostEstimate(
        flops=flops, bytes_accessed=bytes_accessed, transcendentals=transcendentals
    )


def add_angles(first, second):
    return (
        first[0] * second[0] - first[1] * second[1],
        first[1] * second[0] + first[0] * second[1],
    )


def rotated(head, cosine, sine_signed):
    return head * cosine + pltpu.roll(head, HD // 2, 1) * sine_signed


def signed(sine):
    lane = lax.broadcasted_iota(jnp.int32, sine.shape, 1)
    return jnp.where(lane < HD // 2, -sine, sine)


def dot(a, b):
    return jnp.dot(a, b, preferred_element_type=f32)


def dot_t(a, b):
    return lax.dot_general(a, b, (((1,), (1,)), ((), ())), preferred_element_type=f32)


def lane_folded(values):
    total = values[:, :HD]
    for part in range(1, values.shape[1] // HD):
        total = total + values[:, part * HD : (part + 1) * HD]
    return total


def squares_to_factor(squares):
    mean = jnp.sum(squares, axis=-1, keepdims=True) * (1.0 / D)
    return lax.rsqrt(mean + epsilon)


smem = pl.BlockSpec(memory_space=pltpu.SMEM)
vmem = pl.BlockSpec(memory_space=pltpu.VMEM)
anywhere = pl.BlockSpec(memory_space=pl.ANY)


def with_ones(values):
    return jnp.concatenate([values, jnp.ones_like(values)], axis=1)


def slab(to_y, to_c):
    return pl.ds(pl.multiple_of((lax.rem(to_y, NY) * NC + to_c) * FEAT, FEAT), FEAT)


def projection_kernel(
    len_ref, x_hbm, question_hbm, gain_ref, wq_hbm, wk_hbm, wv_hbm, ct_ref, st_ref, cb_ref, sb_ref,
    q_ref, kv_ref, queries_ref, own_ref,
    x_ref, question_ref, wq_ref, wk_ref, wv_ref, scaled_ref, acc_ref, sq_ref, sems, question_sem,
):
    blk_at = lax.axis_index("blk")
    steps = D // KC
    width = HEADS * HD

    def copies(k):
        part = pl.ds(pl.multiple_of(k * KC, KC), KC)
        return [
            pltpu.make_async_copy(x_hbm.at[:, part], x_ref.at[:, part], sems.at[k, 0]),
            pltpu.make_async_copy(wq_hbm.at[part, :], wq_ref.at[part, :], sems.at[k, 1]),
            pltpu.make_async_copy(wk_hbm.at[part, :], wk_ref.at[part, :], sems.at[k, 2]),
            pltpu.make_async_copy(wv_hbm.at[part, :], wv_ref.at[part, :], sems.at[k, 3]),
        ]

    question_copy = pltpu.make_async_copy(question_hbm, question_ref, question_sem)
    question_copy.start()
    for k in range(3):
        for copy in copies(k):
            copy.start()
    acc_ref[...] = jnp.zeros_like(acc_ref)
    sq_ref[...] = jnp.zeros_like(sq_ref)
    question_copy.wait()

    def turn(k, _):
        for copy in copies(k):
            copy.wait()

        @pl.when(k + 3 < steps)
        def _():
            for copy in copies(k + 3):
                copy.start()

        part = pl.ds(pl.multiple_of(k * KC, KC), KC)
        gain = gain_ref[:, part]
        x = x_ref[:, part].astype(f32)
        sq_ref[:BLK] += lane_folded(x * x)
        scaled_ref[:BLK] = (x * gain).astype(bf16)
        x = question_ref[:, part].astype(f32)
        x = jnp.concatenate([x, jnp.zeros((QPAD - QROWS, KC), f32)], 0)
        sq_ref[BLK:] += lane_folded(x * x)
        scaled_ref[BLK:] = (x * gain).astype(bf16)
        acc_ref[:, :width] += dot(scaled_ref[...], wq_ref[part, :])
        acc_ref[:, width:] += dot(scaled_ref[...], jnp.concatenate([wk_ref[part, :], wv_ref[part, :]], axis=1))
        return 0

    lax.fori_loop(0, steps, turn, 0)

    factor = squares_to_factor(sq_ref[...])
    block = pl.ds(blk_at, 1)
    tokens = (ct_ref[...], st_ref[...])
    cosine, sine = add_angles(tokens, (cb_ref[block, :], sb_ref[block, :]))
    total = len_ref[0]
    for b in range(1, N_BLK):
        total = total + len_ref[b]
    high, low = pl.ds(total // BLK, 1), pl.ds(lax.rem(total, BLK), 1)
    base = add_angles((cb_ref[high, :], sb_ref[high, :]), (ct_ref[low, :], st_ref[low, :]))
    rows = pl.ds(pl.multiple_of(blk_at * QROWS, QROWS), QROWS)
    own_cosine, own_sine = add_angles((ct_ref[rows, :], st_ref[rows, :]), base)

    def heads_of(rows, cosine, sine):
        scale = factor[rows]
        cosine, sine = cosine * scale, signed(sine) * scale
        heads = [acc_ref[rows, h * HD : (h + 1) * HD] for h in range(HEADS + 2)]
        turned = [rotated(head, cosine, sine) for head in heads[: HEADS + 1]]
        return [head * q_scale for head in turned[:HEADS]], turned[HEADS], heads[HEADS + 1] * scale

    queries, key, value = heads_of(slice(0, BLK), cosine, sine)
    for h in range(HEADS):
        q_ref[h] = queries[h].astype(bf16)
    kv_ref[:, :HD] = key.astype(bf16)
    kv_ref[:, HD:] = value.astype(bf16)
    queries, key, value = heads_of(slice(BLK, BLK + QROWS), own_cosine, own_sine)
    own_ref[:, :HD] = key.astype(bf16)
    own_ref[:, HD:] = value.astype(bf16)
    queries = jnp.concatenate(queries, axis=1).astype(bf16)
    for b in range(N_BLK):
        queries_ref[b] = queries


def projections(block_len, context, question, gain, wq, wk, wv, tables):
    return pl.pallas_call(
        projection_kernel,
        in_specs=[smem, anywhere, anywhere, vmem, anywhere, anywhere, anywhere] + [vmem] * 4,
        out_specs=[vmem] * 4,
        out_shape=[
            jax.ShapeDtypeStruct((HEADS, BLK, HD), bf16),
            jax.ShapeDtypeStruct((BLK, 2 * HD), bf16),
            jax.ShapeDtypeStruct((N_BLK, QROWS, HEADS * HD), bf16),
            jax.ShapeDtypeStruct((QROWS, 2 * HD), bf16),
        ],
        scratch_shapes=[
            pltpu.VMEM((BLK, D), bf16),
            pltpu.VMEM((QROWS, D), bf16),
            pltpu.VMEM((D, HEADS * HD), bf16),
            pltpu.VMEM((D, HD), bf16),
            pltpu.VMEM((D, HD), bf16),
            pltpu.VMEM((BLK + QPAD, KC), bf16),
            pltpu.VMEM((BLK + QPAD, (HEADS + 2) * HD), f32),
            pltpu.VMEM((BLK + QPAD, HD), f32),
            pltpu.SemaphoreType.DMA((D // KC, 4)),
            pltpu.SemaphoreType.DMA,
        ],
        compiler_params=params(60),
        cost_estimate=cost(2 * BLK * D * 768, 12 * 2**20),
        name="projections",
    )(block_len, context, question, gain, wq, wk, wv, *tables)


def columns_kernel(w_hbm, _, keep_ref, send_ref, sems):
    kv_at = lax.axis_index("kv")
    y_at, c_at = kv_at // NC, lax.rem(kv_at, NC)
    copies = [
        pltpu.make_async_copy(w_hbm.at[:, slab(y_at + d, to_c)], target.at[d], sems.at[i, d])
        for i, (target, to_c) in enumerate(((send_ref, 1 - c_at), (keep_ref, c_at)))
        for d in range(NY)
    ]
    for copy in copies:
        copy.start()
    for copy in copies:
        copy.wait()


def columns(w_out, after):
    return pl.pallas_call(
        columns_kernel,
        in_specs=[anywhere] * 2,
        out_specs=[vmem] * 2,
        out_shape=[jax.ShapeDtypeStruct((NY, HEADS * HD, FEAT), bf16)] * 2,
        scratch_shapes=[pltpu.SemaphoreType.DMA((2, NY))],
        compiler_params=params(60),
        cost_estimate=cost(0, 8 * 2**20),
        name="columns",
    )(w_out, after)


def own_kernel(q_ref, kv_ref, _, o_ref, lse_ref):
    row = lax.broadcasted_iota(jnp.int32, (ROWS, ROWS), 0)
    column = lax.broadcasted_iota(jnp.int32, (ROWS, ROWS), 1)
    causal = column <= row
    for h in range(HEADS):
        for r in range(BLK // ROWS):
            rows = slice(r * ROWS, (r + 1) * ROWS)
            q = q_ref[h, rows, :]
            diagonal = dot_t(q, kv_ref[rows, :HD])
            diagonal = jnp.where(causal, diagonal, masked_score)
            highest = jnp.max(diagonal, axis=-1, keepdims=True)
            if r:
                earlier = dot_t(q, kv_ref[: r * ROWS, :HD])
                highest = jnp.maximum(highest, jnp.max(earlier, axis=-1, keepdims=True))
            weights = jnp.exp2(diagonal - highest).astype(bf16)
            mixture = dot(weights, with_ones(kv_ref[rows, HD:]))
            if r:
                weights = jnp.exp2(earlier - highest).astype(bf16)
                mixture = mixture + dot(weights, with_ones(kv_ref[: r * ROWS, HD:]))
            totals = mixture[:, HD:]
            o_ref[h, rows, :] = mixture[:, :HD] / totals
            lse_ref[h, rows, :] = highest + jnp.log(totals) * log2_e


def own_attention(q, kv, after):
    return pl.pallas_call(
        own_kernel,
        out_shape=[jax.ShapeDtypeStruct((HEADS, BLK, HD), f32)] * 2,
        in_specs=[vmem, vmem, anywhere],
        out_specs=[vmem] * 2,
        compiler_params=params(),
        cost_estimate=cost(HEADS * BLK * BLK * HD * 8, 3 * 2**20, HEADS * BLK * BLK),
        name="own_attention",
    )(q, kv, after)


def question_attention_kernel(len_ref, queries_ref, kv_ref, own_ref, out_ref):
    blk_at = lax.axis_index("blk")
    live = lax.broadcasted_iota(jnp.int32, (QN, BLK), 1) < len_ref[blk_at]
    question_id = lax.broadcasted_iota(jnp.int32, (QN, HD), 0)
    lane = lax.broadcasted_iota(jnp.int32, (QN, HD), 1)
    seen = (lane < QROWS) & (lane + blk_at * QROWS <= question_id)
    own = jnp.concatenate([own_ref[...].astype(f32), jnp.zeros((HD - QROWS, 2 * HD), f32)], 0)
    own = own.astype(bf16)
    values = with_ones(kv_ref[:, HD:])
    own_values = with_ones(own[:, HD:])
    tile = jnp.zeros((QN, HD), f32)
    for h in range(HEADS):
        cols = slice(h * HD, (h + 1) * HD)
        q = queries_ref[:, :, cols].reshape(QN, HD)
        scores = jnp.where(live, dot_t(q, kv_ref[:, :HD]), masked_score)
        own_scores = jnp.where(seen, dot_t(q, own[:, :HD]), masked_score)
        highest = jnp.maximum(
            jnp.max(scores, axis=-1, keepdims=True), jnp.max(own_scores, axis=-1, keepdims=True)
        )
        mixture = dot(jnp.exp2(scores - highest).astype(bf16), values)
        mixture = mixture + dot(jnp.exp2(own_scores - highest).astype(bf16), own_values)
        totals = mixture[:, HD:]
        out_ref[:, :, cols] = (mixture[:, :HD] / totals).reshape(N_BLK, QROWS, HD).astype(bf16)
        lse = highest + jnp.log(totals) * log2_e
        tile = jnp.where(lane // 32 == h, lse, tile)
    high = tile.astype(bf16).astype(f32)
    rest = tile - high
    middle = rest.astype(bf16).astype(f32)
    piece = lane % 32
    pieces = jnp.where(
        piece == 0, high, jnp.where(piece == 1, middle, jnp.where(piece == 2, rest - middle, 0.0))
    )
    out_ref[:, :, HEADS * HD :] = pieces.reshape(N_BLK, QROWS, HD).astype(bf16)


def question_attention(block_len, queries, kv, own):
    return pl.pallas_call(
        question_attention_kernel,
        out_shape=jax.ShapeDtypeStruct((N_BLK, QROWS, (HEADS + 1) * HD), bf16),
        in_specs=[smem] + [vmem] * 3,
        out_specs=vmem,
        compiler_params=params(),
        cost_estimate=cost(HEADS * QN * 640 * HD * 8, 2**20, HEADS * QN * 640),
        name="question_attention",
    )(block_len, queries, kv, own)


def merge_kernel(qlen_ref, parts_ref, _, out_ref):
    parts = parts_ref[...].astype(f32)
    row = lax.broadcasted_iota(jnp.int32, (QROWS, HD), 0) + lax.axis_index("blk") * QROWS
    valid = row < qlen_ref[0]
    stats = parts[:, :, HEADS * HD :]
    heads = []
    for h in range(HEADS):
        at = h * 32
        lse = (stats[:, :, at : at + 1] + stats[:, :, at + 1 : at + 2]) + stats[:, :, at + 2 : at + 3]
        top = jnp.max(lse, axis=0, keepdims=True)
        share = jnp.exp2(lse - top)
        mixture = jnp.sum(parts[:, :, h * HD : (h + 1) * HD] * share, axis=0)
        heads.append(jnp.where(valid, mixture / jnp.sum(share, axis=0), 0.0))
    rows = jnp.concatenate(heads, axis=1)
    out_ref[...] = jnp.concatenate(
        [rows, jnp.zeros((QPAD - QROWS, HEADS * HD), f32)], 0
    ).astype(bf16)


def merge_questions(question_len, parts, after):
    return pl.pallas_call(
        merge_kernel,
        in_specs=[smem, vmem, anywhere],
        out_specs=vmem,
        out_shape=jax.ShapeDtypeStruct((QPAD, HEADS * HD), bf16),
        compiler_params=params(),
        cost_estimate=cost(QN * 640 * 8, 2**19),
        name="merge_questions",
    )(question_len, parts, after)


def context_kernel(
    len_ref, q_ref, o_ref, lse_ref, akv_ref, att_ref
):
    blk_at = lax.axis_index("blk")
    first = blk_at == 0
    values = with_ones(akv_ref[:, HD:])
    for r in range(BLK // ROWS):
        rows = slice(r * ROWS, (r + 1) * ROWS)
        valid = lax.broadcasted_iota(jnp.int32, (ROWS, HD), 0) + r * ROWS < len_ref[blk_at]
        for h in range(HEADS):
            scores = dot_t(q_ref[h, rows, :], akv_ref[:, :HD])
            highest = jnp.max(scores, axis=-1, keepdims=True)
            mixture = dot(jnp.exp2(scores - highest).astype(bf16), values)
            own_lse = lse_ref[h, rows, :]
            top = jnp.where(first, own_lse, jnp.maximum(own_lse, highest))
            own_part = jnp.exp2(own_lse - top)
            anchor_part = jnp.where(first, 0.0, jnp.exp2(jnp.minimum(highest - top, 0.0)))
            result = (o_ref[h, rows, :] * own_part + mixture[:, :HD] * anchor_part) / (
                own_part + mixture[:, HD:] * anchor_part
            )
            att_ref[rows, h * HD : (h + 1) * HD] = jnp.where(valid, result, 0.0).astype(bf16)


def context_attention(block_len, q, own_o, own_lse, anchor):
    return pl.pallas_call(
        context_kernel,
        in_specs=[smem] + [vmem] * 4,
        out_specs=vmem,
        out_shape=jax.ShapeDtypeStruct((BLK, HEADS * HD), bf16),
        compiler_params=params(),
        cost_estimate=cost(HEADS * BLK * BLK * HD * 8 * 20, 4 * 2**20, HEADS * BLK * BLK),
        name="context_attention",
    )(block_len, q, own_o, own_lse, anchor)


def output_kernel(shares, *refs):
    rows_refs, (w_ref, w_other_ref), outs = refs[:4], refs[4:6], refs[6:-2]
    att_ref, other_ref = refs[-2:]
    for i, target in enumerate((att_ref, other_ref)):
        target[:BLK] = rows_refs[2 * i][...]
        target[BLK:] = rows_refs[2 * i + 1][...]
    for i, d in enumerate(shares):
        share = (dot(att_ref[...], w_ref[d]) + dot(other_ref[...], w_other_ref[d])).astype(bf16)
        if len(shares) == 1:
            outs[0][...] = share[:FIRST]
            outs[1][...] = share[FIRST:]
        else:
            outs[i][...] = share


def output_projection(shares, *operands):
    split = (FIRST, ALL_ROWS - FIRST) if len(shares) == 1 else (ALL_ROWS,) * len(shares)
    return pl.pallas_call(
        functools.partial(output_kernel, shares),
        in_specs=[vmem] * 6,
        out_specs=[vmem] * len(split),
        out_shape=[jax.ShapeDtypeStruct((rows, FEAT), bf16) for rows in split],
        scratch_shapes=[pltpu.VMEM((ALL_ROWS, HEADS * HD), bf16)] * 2,
        compiler_params=params(),
        cost_estimate=cost(4 * ALL_ROWS * HEADS * HD * FEAT * len(shares), 3 * 2**20),
        name="output_projection",
    )(*operands)


def relay_kernel(near_ref, far_ref, first_ref, second_ref, near_out, far_out):
    near_out[:FIRST] = (near_ref[:FIRST].astype(f32) + first_ref[...].astype(f32)).astype(bf16)
    near_out[FIRST:] = near_ref[FIRST:]
    far_out[:FIRST] = far_ref[:FIRST]
    far_out[FIRST:] = (far_ref[FIRST:].astype(f32) + second_ref[...].astype(f32)).astype(bf16)


def relay(near, far, first, second):
    return pl.pallas_call(
        relay_kernel,
        in_specs=[vmem] * 4,
        out_specs=[vmem] * 2,
        out_shape=[jax.ShapeDtypeStruct((ALL_ROWS, FEAT), bf16)] * 2,
        compiler_params=params(),
        cost_estimate=cost(ALL_ROWS * FEAT, ALL_ROWS * FEAT * 10),
        name="relay",
    )(near, far, first, second)


def finish_kernel(own_ref, left_ref, right_ref, out_ref, question_ref):
    total = own_ref[...].astype(f32) + left_ref[...].astype(f32) + right_ref[...].astype(f32)
    out_ref[...] = total[:BLK].astype(bf16)
    question_ref[...] = total[BLK : BLK + QROWS].astype(bf16)


def finish(own, left, right):
    return pl.pallas_call(
        finish_kernel,
        in_specs=[vmem] * 3,
        out_specs=[vmem] * 2,
        out_shape=[
            jax.ShapeDtypeStruct((BLK, FEAT), bf16),
            jax.ShapeDtypeStruct((QROWS, FEAT), bf16),
        ],
        compiler_params=params(),
        cost_estimate=cost(BLK * FEAT * 3, BLK * FEAT * 8),
        name="finish",
    )(own, left, right)


def sum_kernel(*refs):
    total = refs[0][...].astype(f32)
    for ref in refs[1:-2]:
        total = total + ref[...].astype(f32)
    refs[-1][...] = total.astype(bf16)


def sum_of(*parts, after):
    return pl.pallas_call(
        sum_kernel,
        in_specs=[vmem] * len(parts) + [anywhere],
        out_specs=vmem,
        out_shape=jax.ShapeDtypeStruct(parts[0].shape, bf16),
        compiler_params=params(),
        cost_estimate=cost(BLK * 256 * 3, BLK * 256 * 8),
        name="sum_of",
    )(*parts, after)


def shift_y(value, by):
    pairs = [(y * NC + c, (y + by) % NY * NC + c) for y in range(NY) for c in range(NC)]
    return lax.ppermute(value, "kv", pairs)


def swap_cores(value):
    pairs = [(y * NC + c, y * NC + 1 - c) for y in range(NY) for c in range(NC)]
    return lax.ppermute(value, "kv", pairs)


def body(context, question, norm_gain, w_query, w_key, w_value, w_out, block_len, question_len):
    blk_at = lax.axis_index("blk")
    tables = [jnp.asarray(t) for t in angle_tables(np.arange(BLK))]
    tables += [jnp.asarray(t) for t in angle_tables(np.arange(N_BLK + 1) * BLK)]

    q, kv, queries, own_kv = projections(
        block_len, context, question, norm_gain.reshape(1, D), w_query, w_key, w_value, tables
    )
    held = jnp.where(blk_at == 0, kv, jnp.zeros_like(kv))
    held = held + lax.ppermute(kv, "blk", [(0, 3)]) + lax.ppermute(kv, "blk", [(0, 5)])
    queries = lax.all_to_all(queries, "blk", 0, 0)
    w_keep, w_send = columns(w_out, held)
    own_o, own_lse = own_attention(q, kv, w_send)
    w_other = swap_cores(w_send)
    second = lax.ppermute(held, "blk", [(0, 1), (3, 4), (5, 6)])
    third = lax.ppermute(held, "blk", [(0, 7), (3, 2)])
    held = sum_of(held, second, third, after=own_o)
    anchor = jnp.where(blk_at < NZ, held, jnp.zeros_like(held))
    for x in range(1, NX):
        anchor = anchor + lax.ppermute(held, "blk", [(z, x * NZ + z) for z in range(NZ)])
    parts = question_attention(block_len, queries, kv, own_kv)
    parts = lax.all_to_all(parts, "blk", 0, 0)

    rows = context_attention(block_len, q, own_o, own_lse, anchor)
    other_rows = swap_cores(rows)
    questions = merge_questions(question_len, parts, rows)
    operands = (rows, questions, other_rows, swap_cores(questions), w_keep, w_other)
    across = output_projection((2,), *operands)
    first, second = shift_y(across[0], 1), shift_y(across[1], 3)
    near, far, own = output_projection((1, 3, 0), *operands)
    near, far = relay(near, far, first, second)
    return finish(own, shift_y(near, 1), shift_y(far, 3))


def solution(mesh):
    return jax.shard_map(
        body,
        mesh=mesh,
        in_specs=(
            P("blk", None),
            P("blk", None),
            P(),
            P(None, "kv"),
            P(None, "kv"),
            P(None, "kv"),
            P("kv", None),
            P(),
            P(),
        ),
        out_specs=(P("blk", "kv"), P("blk", "kv")),
        check_vma=False,
    )
```

```python
import functools

import jax
import jax.numpy as jnp
import numpy as np
from jax import lax
from jax.experimental import pallas as pl
from jax.experimental.pallas import tpu as pltpu
from jax.sharding import PartitionSpec as P

HD = 128
HEADS = 4
BLK = 512
QROWS = 8
NX, NZ, NY, NC = 4, 8, 4, 2
N_BLK, N_KV = NX * NZ, NY * NC
QN = N_BLK * QROWS
D = 4096
FEAT = D // N_KV
KC = 1024
ROWS = 256
QPAD = 16
CONTEXT_LIMIT = 58

epsilon = 1e-05
rope_base = 500000.0
masked_score = -1e30
q_scale = float(HD**-0.5 * np.log2(np.e))
log2_e = float(np.log2(np.e))

bf16 = jnp.bfloat16
f32 = jnp.float32


def angle_tables(positions):
    inverse_freq = rope_base ** (-2.0 * np.arange(HD // 2, dtype=np.float64) / HD)
    angles = np.asarray(positions, np.float64)[:, None] * inverse_freq[None, :]
    angles = np.concatenate([angles, angles], 1)
    return np.cos(angles).astype(np.float32), np.sin(angles).astype(np.float32)


def params(limit=24):
    return pltpu.CompilerParams(vmem_limit_bytes=limit * 2**20)


def cost(flops, bytes_accessed, transcendentals=0):
    return pl.CostEstimate(
        flops=flops, bytes_accessed=bytes_accessed, transcendentals=transcendentals
    )


def add_angles(first, second):
    return (
        first[0] * second[0] - first[1] * second[1],
        first[1] * second[0] + first[0] * second[1],
    )


def rotated(head, cosine, sine_signed):
    return head * cosine + pltpu.roll(head, HD // 2, 1) * sine_signed


def signed(sine):
    lane = lax.broadcasted_iota(jnp.int32, sine.shape, 1)
    return jnp.where(lane < HD // 2, -sine, sine)


def dot(a, b):
    return jnp.dot(a, b, preferred_element_type=f32)


def dot_t(a, b):
    return lax.dot_general(a, b, (((1,), (1,)), ((), ())), preferred_element_type=f32)


def lane_folded(values):
    total = values[:, :HD]
    for part in range(1, values.shape[1] // HD):
        total = total + values[:, part * HD : (part + 1) * HD]
    return total


def squares_to_factor(squares):
    mean = jnp.sum(squares, axis=-1, keepdims=True) * (1.0 / D)
    return lax.rsqrt(mean + epsilon)


smem = pl.BlockSpec(memory_space=pltpu.SMEM)
vmem = pl.BlockSpec(memory_space=pltpu.VMEM)
anywhere = pl.BlockSpec(memory_space=pl.ANY)


def with_ones(values):
    return jnp.concatenate([values, jnp.ones_like(values)], axis=1)


def projection_kernel(
    len_ref, x_hbm, question_hbm, gain_ref, wq_hbm, wk_hbm, wv_hbm, ct_hbm, st_hbm, cb_ref, sb_ref,
    q_ref, kv_ref, queries_ref, own_ref, ct_ref, st_ref, table_sems,
    x_ref, question_ref, wq_ref, wk_ref, wv_ref, scaled_ref, acc_ref, sq_ref, sems, question_sem,
):
    blk_at = lax.axis_index("blk")
    steps = D // KC
    width = HEADS * HD

    def copies(k):
        part = pl.ds(pl.multiple_of(k * KC, KC), KC)
        return [
            pltpu.make_async_copy(x_hbm.at[:, part], x_ref.at[:, part], sems.at[k, 0]),
            pltpu.make_async_copy(wq_hbm.at[part, :], wq_ref.at[part, :], sems.at[k, 1]),
            pltpu.make_async_copy(wk_hbm.at[part, :], wk_ref.at[part, :], sems.at[k, 2]),
            pltpu.make_async_copy(wv_hbm.at[part, :], wv_ref.at[part, :], sems.at[k, 3]),
        ]

    question_copy = pltpu.make_async_copy(question_hbm, question_ref, question_sem)
    question_copy.start()
    for k in range(2):
        for copy in copies(k):
            copy.start()
    table_copies = [
        pltpu.make_async_copy(ct_hbm, ct_ref, table_sems.at[0]),
        pltpu.make_async_copy(st_hbm, st_ref, table_sems.at[1]),
    ]
    for copy in table_copies:
        copy.start()
    acc_ref[...] = jnp.zeros_like(acc_ref)
    sq_ref[...] = jnp.zeros_like(sq_ref)
    question_copy.wait()

    def turn(k, _):
        for copy in copies(k):
            copy.wait()

        @pl.when(k + 2 < steps)
        def _():
            for copy in copies(k + 2):
                copy.start()

        part = pl.ds(pl.multiple_of(k * KC, KC), KC)
        gain = gain_ref[:, part]
        x = x_ref[:, part].astype(f32)
        sq_ref[:BLK] += lane_folded(x * x)
        scaled_ref[:BLK] = (x * gain).astype(bf16)
        x = question_ref[:, part].astype(f32)
        x = jnp.concatenate([x, jnp.zeros((QPAD - QROWS, KC), f32)], 0)
        sq_ref[BLK:] += lane_folded(x * x)
        scaled_ref[BLK:] = (x * gain).astype(bf16)
        acc_ref[:, :width] += dot(scaled_ref[...], wq_ref[part, :])
        acc_ref[:, width:] += dot(scaled_ref[...], jnp.concatenate([wk_ref[part, :], wv_ref[part, :]], axis=1))
        return 0

    lax.fori_loop(0, steps, turn, 0)
    for copy in table_copies:
        copy.wait()

    factor = squares_to_factor(sq_ref[...])
    block = pl.ds(blk_at, 1)
    tokens = (ct_ref[...], st_ref[...])
    cosine, sine = add_angles(tokens, (cb_ref[block, :], sb_ref[block, :]))
    total = len_ref[0]
    for b in range(1, N_BLK):
        total = total + len_ref[b]
    high, low = pl.ds(total // BLK, 1), pl.ds(lax.rem(total, BLK), 1)
    base = add_angles((cb_ref[high, :], sb_ref[high, :]), (ct_ref[low, :], st_ref[low, :]))
    rows = pl.ds(pl.multiple_of(blk_at * QROWS, QROWS), QROWS)
    own_cosine, own_sine = add_angles((ct_ref[rows, :], st_ref[rows, :]), base)

    def heads_of(rows, cosine, sine):
        scale = factor[rows]
        cosine, sine = cosine * scale, signed(sine) * scale
        heads = [acc_ref[rows, h * HD : (h + 1) * HD] for h in range(HEADS + 2)]
        turned = [rotated(head, cosine, sine) for head in heads[: HEADS + 1]]
        return [head * q_scale for head in turned[:HEADS]], turned[HEADS], heads[HEADS + 1] * scale

    queries, key, value = heads_of(slice(0, BLK), cosine, sine)
    for h in range(HEADS):
        q_ref[h] = queries[h].astype(bf16)
    kv_ref[:, :HD] = key.astype(bf16)
    kv_ref[:, HD:] = value.astype(bf16)
    queries, key, value = heads_of(slice(BLK, BLK + QROWS), own_cosine, own_sine)
    own_ref[:, :HD] = key.astype(bf16)
    own_ref[:, HD:] = value.astype(bf16)
    queries = jnp.concatenate(queries, axis=1).astype(bf16)
    for b in range(N_BLK):
        queries_ref[b] = queries


def projections(block_len, context, question, gain, wq, wk, wv, tables):
    return pl.pallas_call(
        projection_kernel,
        in_specs=[smem, anywhere, anywhere, vmem] + [anywhere] * 5 + [vmem] * 2,
        out_specs=[vmem] * 4,
        out_shape=[
            jax.ShapeDtypeStruct((HEADS, BLK, HD), bf16),
            jax.ShapeDtypeStruct((BLK, 2 * HD), bf16),
            jax.ShapeDtypeStruct((N_BLK, QROWS, HEADS * HD), bf16),
            jax.ShapeDtypeStruct((QROWS, 2 * HD), bf16),
        ],
        scratch_shapes=[
            pltpu.VMEM((BLK, HD), f32),
            pltpu.VMEM((BLK, HD), f32),
            pltpu.SemaphoreType.DMA((2,)),
            pltpu.VMEM((BLK, D), bf16),
            pltpu.VMEM((QROWS, D), bf16),
            pltpu.VMEM((D, HEADS * HD), bf16),
            pltpu.VMEM((D, HD), bf16),
            pltpu.VMEM((D, HD), bf16),
            pltpu.VMEM((BLK + QPAD, KC), bf16),
            pltpu.VMEM((BLK + QPAD, (HEADS + 2) * HD), f32),
            pltpu.VMEM((BLK + QPAD, HD), f32),
            pltpu.SemaphoreType.DMA((D // KC, 4)),
            pltpu.SemaphoreType.DMA,
        ],
        compiler_params=params(60),
        cost_estimate=cost(2 * BLK * D * 768, 12 * 2**20),
        name="projections",
    )(block_len, context, question, gain, wq, wk, wv, *tables)


def question_attention_kernel(len_ref, queries_ref, kv_ref, own_ref, out_ref, token_ref):
    token_ref[...] = jnp.zeros_like(token_ref)
    blk_at = lax.axis_index("blk")
    live = lax.broadcasted_iota(jnp.int32, (QN, BLK), 1) < len_ref[blk_at]
    question_id = lax.broadcasted_iota(jnp.int32, (QN, HD), 0)
    lane = lax.broadcasted_iota(jnp.int32, (QN, HD), 1)
    seen = (lane < QROWS) & (lane + blk_at * QROWS <= question_id)
    own = jnp.concatenate([own_ref[...].astype(f32), jnp.zeros((HD - QROWS, 2 * HD), f32)], 0)
    own = own.astype(bf16)
    values = with_ones(kv_ref[:, HD:])
    own_values = with_ones(own[:, HD:])
    tile = jnp.zeros((QN, HD), f32)
    for h in range(HEADS):
        cols = slice(h * HD, (h + 1) * HD)
        q = queries_ref[:, :, cols].reshape(QN, HD)
        scores = jnp.where(live, dot_t(q, kv_ref[:, :HD]), masked_score)
        own_scores = jnp.where(seen, dot_t(q, own[:, :HD]), masked_score)
        highest = jnp.maximum(
            jnp.max(scores, axis=-1, keepdims=True), jnp.max(own_scores, axis=-1, keepdims=True)
        )
        mixture = dot(jnp.exp2(scores - highest).astype(bf16), values)
        mixture = mixture + dot(jnp.exp2(own_scores - highest).astype(bf16), own_values)
        totals = mixture[:, HD:]
        out_ref[:, :, cols] = (mixture[:, :HD] / totals).reshape(N_BLK, QROWS, HD)
        lse = highest + jnp.log(totals) * log2_e
        tile = jnp.where(lane // 32 == h, lse, tile)
    out_ref[:, :, HEADS * HD :] = tile.reshape(N_BLK, QROWS, HD)


def question_attention(block_len, queries, kv, own):
    return pl.pallas_call(
        question_attention_kernel,
        out_shape=[
            jax.ShapeDtypeStruct((N_BLK, QROWS, (HEADS + 1) * HD), f32),
            jax.ShapeDtypeStruct((8, HD), f32),
        ],
        in_specs=[smem] + [vmem] * 3,
        out_specs=[vmem] * 2,
        compiler_params=params(),
        cost_estimate=cost(HEADS * QN * 640 * HD * 8, 2**20, HEADS * QN * 640),
        name="question_attention",
    )(block_len, queries, kv, own)


def merged(qlen_ref, parts_ref):
    row = lax.broadcasted_iota(jnp.int32, (QROWS, HD), 0) + lax.axis_index("blk") * QROWS
    valid = row < qlen_ref[0]
    heads = []
    for h in range(HEADS):
        lse = parts_ref[:, :, HEADS * HD + h * 32 : HEADS * HD + h * 32 + 1]
        top = jnp.max(lse, axis=0, keepdims=True)
        share = jnp.exp2(lse - top)
        mixture = jnp.sum(parts_ref[:, :, h * HD : (h + 1) * HD] * share, axis=0)
        heads.append(jnp.where(valid, mixture / jnp.sum(share, axis=0), 0.0))
    rows = jnp.concatenate(heads, axis=1)
    return jnp.concatenate([rows, jnp.zeros((QPAD - QROWS, HEADS * HD), f32)], 0).astype(bf16)


def context_kernel(
    len_ref, q_ref, kv_ref, akv_ref, w_hbm, _, *refs
):
    keep_refs, send_refs, (att_ref, w_ref, sem) = refs[:NY], refs[NY : 2 * NY], refs[2 * NY :]
    blk_at, kv_at = lax.axis_index("blk"), lax.axis_index("kv")
    y_at, c_at = kv_at // NC, lax.rem(kv_at, NC)
    copy = pltpu.make_async_copy(w_hbm, w_ref, sem)
    copy.start()
    first = blk_at == 0
    row = lax.broadcasted_iota(jnp.int32, (ROWS, ROWS), 0)
    causal = lax.broadcasted_iota(jnp.int32, (ROWS, ROWS), 1) <= row
    anchor_values = with_ones(akv_ref[:, HD:])
    values = with_ones(kv_ref[:, HD:])
    for r in range(BLK // ROWS):
        rows, before = slice(r * ROWS, (r + 1) * ROWS), slice(0, r * ROWS)
        valid = lax.broadcasted_iota(jnp.int32, (ROWS, HD), 0) + r * ROWS < len_ref[blk_at]
        for h in range(HEADS):
            q = q_ref[h, rows, :]
            anchor = dot_t(q, akv_ref[:, :HD])
            own = [jnp.where(causal, dot_t(q, kv_ref[rows, :HD]), masked_score)]
            if r:
                own.append(dot_t(q, kv_ref[before, :HD]))
            highest = jnp.max(own[0], axis=-1, keepdims=True)
            for scores in own[1:]:
                highest = jnp.maximum(highest, jnp.max(scores, axis=-1, keepdims=True))
            anchor_highest = jnp.max(anchor, axis=-1, keepdims=True)
            highest = jnp.where(first, highest, jnp.maximum(highest, anchor_highest))
            weights = jnp.exp2(anchor - jnp.where(first, -masked_score, highest))
            mixture = dot(weights.astype(bf16), anchor_values)
            for scores, at in zip(own, (rows, before)):
                mixture = mixture + dot(jnp.exp2(scores - highest).astype(bf16), values[at])
            result = mixture[:, :HD] / mixture[:, HD:]
            att_ref[rows, h * HD : (h + 1) * HD] = jnp.where(valid, result, 0.0).astype(bf16)
    copy.wait()
    for d in range(NY):
        to_y = lax.rem(y_at + d, NY)
        for ref, to_c in ((send_refs[d], 1 - c_at), (keep_refs[d], c_at)):
            columns = pl.ds(pl.multiple_of((to_y * NC + to_c) * FEAT, FEAT), FEAT)
            ref[...] = dot(att_ref[...], w_ref[:, columns]).astype(bf16)


def context_attention(block_len, q, kv, anchor, w_out, after):
    return pl.pallas_call(
        context_kernel,
        in_specs=[smem] + [vmem] * 3 + [anywhere] * 2,
        out_specs=[vmem] * (2 * NY),
        out_shape=[jax.ShapeDtypeStruct((BLK, FEAT), bf16)] * (2 * NY),
        scratch_shapes=[
            pltpu.VMEM((BLK, HEADS * HD), bf16),
            pltpu.VMEM((HEADS * HD, D), bf16),
            pltpu.SemaphoreType.DMA,
        ],
        compiler_params=params(CONTEXT_LIMIT),
        cost_estimate=cost(HEADS * BLK * BLK * HD * 8 * 20, 4 * 2**20, HEADS * BLK * BLK),
        name="context_attention",
    )(block_len, q, kv, anchor, w_out, after)


def question_output_kernel(qlen_ref, parts_ref, w_hbm, _, keep_ref, send_ref, w_ref, sem):
    copy = pltpu.make_async_copy(w_hbm, w_ref, sem)
    copy.start()
    kv_at = lax.axis_index("kv")
    y_at, c_at = kv_at // NC, lax.rem(kv_at, NC)
    rows = merged(qlen_ref, parts_ref)
    copy.wait()
    for d in range(NY):
        to_y = lax.rem(y_at + d, NY)
        for ref, to_c in ((send_ref, 1 - c_at), (keep_ref, c_at)):
            columns = pl.ds(pl.multiple_of((to_y * NC + to_c) * FEAT, FEAT), FEAT)
            ref[d] = dot(rows, w_ref[:, columns]).astype(bf16)


def question_output(question_len, parts, w_out, after):
    return pl.pallas_call(
        question_output_kernel,
        in_specs=[smem, vmem] + [anywhere] * 2,
        out_specs=[vmem] * 2,
        out_shape=[jax.ShapeDtypeStruct((NY, QPAD, FEAT), bf16)] * 2,
        scratch_shapes=[pltpu.VMEM((HEADS * HD, D), bf16), pltpu.SemaphoreType.DMA],
        compiler_params=params(CONTEXT_LIMIT),
        cost_estimate=cost(400 * 256 * HEADS * HD * FEAT * NY, 4 * 2**20),
        name="question_output",
    )(question_len, parts, w_out, after)


def total_of(*parts):
    total = parts[0].astype(f32)
    for part in parts[1:]:
        total = total + part.astype(f32)
    return total.astype(bf16)


def across_kernel(keep_ref, got_ref, first_ref, second_ref):
    first_ref[...] = total_of(keep_ref[:ROWS], got_ref[:ROWS])
    second_ref[...] = total_of(keep_ref[ROWS:], got_ref[ROWS:])


def across_sum(keep, got):
    return pl.pallas_call(
        across_kernel,
        in_specs=[vmem] * 2,
        out_specs=[vmem] * 2,
        out_shape=[jax.ShapeDtypeStruct((ROWS, FEAT), bf16)] * 2,
        compiler_params=params(),
        cost_estimate=cost(0, 0),
        name="across_sum",
    )(keep, got)


def others_kernel(near_keep, near_got, far_keep, far_got, near_a, near_b, far_a, far_b):
    near_a[...] = total_of(near_keep[:ROWS], near_got[:ROWS])
    near_b[...] = total_of(near_keep[ROWS:], near_got[ROWS:])
    far_a[...] = total_of(far_keep[:ROWS], far_got[:ROWS])
    far_b[...] = total_of(far_keep[ROWS:], far_got[ROWS:])


def others_sum(*parts):
    return pl.pallas_call(
        others_kernel,
        in_specs=[vmem] * 4,
        out_specs=[vmem] * 4,
        out_shape=[jax.ShapeDtypeStruct((ROWS, FEAT), bf16)] * 4,
        compiler_params=params(),
        cost_estimate=cost(0, 0),
        name="others_sum",
    )(*parts)


def relay_kernel(
    near_ref, far_ref, first_ref, second_ref, q_keep, q_got, _, __,
    near_out, far_out, q_own_out, q_across_out,
):
    near_out[:ROWS] = total_of(near_ref[...], first_ref[...])
    far_out[:ROWS] = total_of(far_ref[...], second_ref[...])
    for d, out in enumerate((q_own_out, near_out.at[ROWS:], q_across_out, far_out.at[ROWS:])):
        out[...] = total_of(q_keep[d], q_got[d])


def relay(*parts):
    half = jax.ShapeDtypeStruct((ROWS + QPAD, FEAT), bf16)
    return pl.pallas_call(
        relay_kernel,
        in_specs=[vmem] * 6 + [anywhere] * 2,
        out_specs=[vmem] * 4,
        out_shape=[half] * 2 + [jax.ShapeDtypeStruct((QPAD, FEAT), bf16)] * 2,
        compiler_params=params(),
        cost_estimate=cost(BLK * FEAT, BLK * FEAT * 10),
        name="relay",
    )(*parts)


def finish_kernel(
    keep, got, left_a, left_b, right_a, right_b, q_own, q_across, out_ref, question_ref
):
    out_ref[:ROWS] = total_of(keep[:ROWS], got[:ROWS], left_a[:ROWS], right_a[...])
    out_ref[ROWS:] = total_of(keep[ROWS:], got[ROWS:], left_b[...], right_b[:ROWS])
    question = total_of(q_own[...], left_a[ROWS:], right_b[ROWS:], q_across[...])
    question_ref[...] = question[:QROWS]


def finish(*parts):
    return pl.pallas_call(
        finish_kernel,
        in_specs=[vmem] * len(parts),
        out_specs=[vmem] * 2,
        out_shape=[
            jax.ShapeDtypeStruct((BLK, FEAT), bf16),
            jax.ShapeDtypeStruct((QROWS, FEAT), bf16),
        ],
        compiler_params=params(),
        cost_estimate=cost(BLK * FEAT * 4, BLK * FEAT * 10),
        name="finish",
    )(*parts)


def sum_kernel(*refs):
    total = refs[0][...].astype(f32)
    for ref in refs[1:-2]:
        total = total + ref[...].astype(f32)
    refs[-1][...] = total.astype(bf16)


def sum_of(*parts, after):
    return pl.pallas_call(
        sum_kernel,
        in_specs=[vmem] * len(parts) + [anywhere],
        out_specs=vmem,
        out_shape=jax.ShapeDtypeStruct(parts[0].shape, bf16),
        compiler_params=params(),
        cost_estimate=cost(BLK * 256 * 3, BLK * 256 * 8),
        name="sum_of",
    )(*parts, after)


def to_blocks(pairs):
    return [(a * NZ + b, c * NZ + d) for (a, b), (c, d) in pairs.items()]


def shift_y(value, by):
    pairs = [(y * NC + c, (y + by) % NY * NC + c) for y in range(NY) for c in range(NC)]
    return lax.ppermute(value, "kv", pairs)


def swap_cores(value):
    pairs = [(y * NC + c, y * NC + 1 - c) for y in range(NY) for c in range(NC)]
    return lax.ppermute(value, "kv", pairs)


def body(context, question, norm_gain, w_query, w_key, w_value, w_out, block_len, question_len):
    blk_at = lax.axis_index("blk")
    tables = [jnp.asarray(t) for t in angle_tables(np.arange(BLK))]
    tables += [jnp.asarray(t) for t in angle_tables(np.arange(N_BLK + 1) * BLK)]

    q, kv, queries, own_kv = projections(
        block_len, context, question, norm_gain.reshape(1, D), w_query, w_key, w_value, tables
    )
    held = jnp.where(blk_at == 0, kv, jnp.zeros_like(kv))
    held = held + lax.ppermute(kv, "blk", to_blocks({(0, 0): (2, 0)}))
    held = held + lax.ppermute(kv, "blk", to_blocks({(0, 0): (0, 3)}))
    held = held + lax.ppermute(kv, "blk", to_blocks({(0, 0): (0, 5)}))
    queries = lax.all_to_all(queries, "blk", 0, 0)
    within = {(0, 0): (0, 1), (0, 3): (0, 4), (0, 5): (0, 6)}, {(0, 0): (0, 7), (0, 3): (0, 2)}
    second = lax.ppermute(held, "blk", to_blocks({**within[0], (2, 0): (2, 3)}))
    third = lax.ppermute(held, "blk", to_blocks({**within[1], (2, 0): (2, 5)}))
    parts, token = question_attention(block_len, queries, kv, own_kv)
    held = sum_of(held, second, third, after=token)
    anchor = held
    for x, pairs in zip((1, 3), within):
        pairs = {(2, a): (2, b) for (_, a), (_, b) in pairs.items()}
        across = {(0, z): (x, z) for z in range(NZ)}
        anchor = anchor + lax.ppermute(held, "blk", to_blocks({**across, **pairs}))
    parts = lax.all_to_all(parts, "blk", 0, 0)

    products = context_attention(block_len, q, kv, anchor, w_out, token)
    keep, send = products[:NY], products[NY:]
    first, second = across_sum(keep[2], swap_cores(send[2]))
    near_a, near_b, far_a, far_b = others_sum(
        keep[1], swap_cores(send[1]), keep[3], swap_cores(send[3])
    )
    left_b, right_a = shift_y(near_b, 1), shift_y(far_a, 3)
    q_keep, q_send = question_output(question_len, parts, w_out, first)
    first, second = shift_y(first, 1), shift_y(second, 3)
    near, far, q_own, q_across = relay(
        near_a, far_b, first, second, q_keep, swap_cores(q_send), left_b, right_a
    )
    left_a, right_b = shift_y(near, 1), shift_y(far, 3)
    q_across = shift_y(q_across, 2)
    own = keep[0], swap_cores(send[0])
    return finish(*own, left_a, left_b, right_a, right_b, q_own, q_across)


def solution(mesh):
    return jax.shard_map(
        body,
        mesh=mesh,
        in_specs=(
            P("blk", None),
            P("blk", None),
            P(),
            P(None, "kv"),
            P(None, "kv"),
            P(None, "kv"),
            P("kv", None),
            P(),
            P(),
        ),
        out_specs=(P("blk", "kv"), P("blk", "kv")),
        check_vma=False,
    )
```

```python
import functools

import jax
import jax.numpy as jnp
import numpy as np
from jax import lax
from jax.experimental import pallas as pl
from jax.experimental.pallas import tpu as pltpu
from jax.sharding import PartitionSpec as P

HD = 128
HEADS = 4
BLK = 512
QROWS = 8
NX, NZ, NY, NC = 4, 8, 4, 2
N_BLK, N_KV = NX * NZ, NY * NC
QN = N_BLK * QROWS
D = 4096
FEAT = D // N_KV
KC = 1024
ROWS = 256
QPAD = 16

epsilon = 1e-05
rope_base = 500000.0
masked_score = -1e30
q_scale = float(HD**-0.5 * np.log2(np.e))
log2_e = float(np.log2(np.e))

bf16 = jnp.bfloat16
f32 = jnp.float32


def angle_tables(positions):
    inverse_freq = rope_base ** (-2.0 * np.arange(HD // 2, dtype=np.float64) / HD)
    angles = np.asarray(positions, np.float64)[:, None] * inverse_freq[None, :]
    angles = np.concatenate([angles, angles], 1)
    return np.cos(angles).astype(np.float32), np.sin(angles).astype(np.float32)


def params(limit=24):
    return pltpu.CompilerParams(vmem_limit_bytes=limit * 2**20)


def cost(flops, bytes_accessed, transcendentals=0):
    return pl.CostEstimate(
        flops=flops, bytes_accessed=bytes_accessed, transcendentals=transcendentals
    )


def add_angles(first, second):
    return (
        first[0] * second[0] - first[1] * second[1],
        first[1] * second[0] + first[0] * second[1],
    )


def rotated(head, cosine, sine_signed):
    return head * cosine + pltpu.roll(head, HD // 2, 1) * sine_signed


def signed(sine):
    lane = lax.broadcasted_iota(jnp.int32, sine.shape, 1)
    return jnp.where(lane < HD // 2, -sine, sine)


def dot(a, b):
    return jnp.dot(a, b, preferred_element_type=f32)


def dot_t(a, b):
    return lax.dot_general(a, b, (((1,), (1,)), ((), ())), preferred_element_type=f32)


def lane_folded(values):
    total = values[:, :HD]
    for part in range(1, values.shape[1] // HD):
        total = total + values[:, part * HD : (part + 1) * HD]
    return total


def squares_to_factor(squares):
    mean = jnp.sum(squares, axis=-1, keepdims=True) * (1.0 / D)
    return lax.rsqrt(mean + epsilon)


smem = pl.BlockSpec(memory_space=pltpu.SMEM)
vmem = pl.BlockSpec(memory_space=pltpu.VMEM)
anywhere = pl.BlockSpec(memory_space=pl.ANY)


def with_ones(values):
    return jnp.concatenate([values, jnp.ones_like(values)], axis=1)


def projection_kernel(
    len_ref, x_hbm, question_hbm, gain_ref, wq_hbm, wk_hbm, wv_hbm, ct_hbm, st_hbm, cb_ref, sb_ref,
    q_ref, kv_ref, queries_ref, ct_ref, st_ref, table_sems,
    x_ref, question_ref, wq_ref, wk_ref, wv_ref, scaled_ref, acc_ref, sq_ref, sems, question_sem,
):
    blk_at = lax.axis_index("blk")
    steps = D // KC
    width = HEADS * HD

    def copies(k):
        part = pl.ds(pl.multiple_of(k * KC, KC), KC)
        return [
            pltpu.make_async_copy(x_hbm.at[:, part], x_ref.at[:, part], sems.at[k, 0]),
            pltpu.make_async_copy(wq_hbm.at[part, :], wq_ref.at[part, :], sems.at[k, 1]),
            pltpu.make_async_copy(wk_hbm.at[part, :], wk_ref.at[part, :], sems.at[k, 2]),
            pltpu.make_async_copy(wv_hbm.at[part, :], wv_ref.at[part, :], sems.at[k, 3]),
        ]

    question_copy = pltpu.make_async_copy(question_hbm, question_ref, question_sem)
    question_copy.start()
    for k in range(2):
        for copy in copies(k):
            copy.start()
    table_copies = [
        pltpu.make_async_copy(ct_hbm, ct_ref, table_sems.at[0]),
        pltpu.make_async_copy(st_hbm, st_ref, table_sems.at[1]),
    ]
    for copy in table_copies:
        copy.start()
    acc_ref[...] = jnp.zeros_like(acc_ref)
    sq_ref[...] = jnp.zeros_like(sq_ref)
    question_copy.wait()

    def turn(k, _):
        for copy in copies(k):
            copy.wait()

        @pl.when(k + 2 < steps)
        def _():
            for copy in copies(k + 2):
                copy.start()

        part = pl.ds(pl.multiple_of(k * KC, KC), KC)
        gain = gain_ref[:, part]
        x = x_ref[:, part].astype(f32)
        sq_ref[:BLK] += lane_folded(x * x)
        scaled_ref[:BLK] = (x * gain).astype(bf16)
        x = question_ref[:, part].astype(f32)
        x = jnp.concatenate([x, jnp.zeros((QPAD - QROWS, KC), f32)], 0)
        sq_ref[BLK:] += lane_folded(x * x)
        scaled_ref[BLK:] = (x * gain).astype(bf16)
        acc_ref[:, :width] += dot(scaled_ref[...], wq_ref[part, :])
        acc_ref[:, width:] += dot(scaled_ref[...], jnp.concatenate([wk_ref[part, :], wv_ref[part, :]], axis=1))
        return 0

    lax.fori_loop(0, steps, turn, 0)
    for copy in table_copies:
        copy.wait()

    factor = squares_to_factor(sq_ref[...])
    block = pl.ds(blk_at, 1)
    tokens = (ct_ref[...], st_ref[...])
    cosine, sine = add_angles(tokens, (cb_ref[block, :], sb_ref[block, :]))
    total = len_ref[0]
    for b in range(1, N_BLK):
        total = total + len_ref[b]
    high, low = pl.ds(total // BLK, 1), pl.ds(lax.rem(total, BLK), 1)
    base = add_angles((cb_ref[high, :], sb_ref[high, :]), (ct_ref[low, :], st_ref[low, :]))
    rows = pl.ds(pl.multiple_of(blk_at * QROWS, QROWS), QROWS)
    own_cosine, own_sine = add_angles((ct_ref[rows, :], st_ref[rows, :]), base)

    def heads_of(rows, cosine, sine):
        scale = factor[rows]
        cosine, sine = cosine * scale, signed(sine) * scale
        heads = [acc_ref[rows, h * HD : (h + 1) * HD] for h in range(HEADS + 2)]
        turned = [rotated(head, cosine, sine) for head in heads[: HEADS + 1]]
        return [head * q_scale for head in turned[:HEADS]], turned[HEADS], heads[HEADS + 1] * scale

    queries, key, value = heads_of(slice(0, BLK), cosine, sine)
    for h in range(HEADS):
        q_ref[h] = queries[h].astype(bf16)
    kv_ref[:BLK, :HD] = key.astype(bf16)
    kv_ref[:BLK, HD:] = value.astype(bf16)
    queries, key, value = heads_of(slice(BLK, BLK + QROWS), own_cosine, own_sine)
    own = jnp.concatenate([key, value], axis=1)
    own = jnp.concatenate([own, jnp.zeros((QPAD - QROWS, 2 * HD), f32)], axis=0)
    kv_ref[BLK:] = own.astype(bf16)
    queries = jnp.concatenate(queries, axis=1).astype(bf16)
    for b in range(N_BLK):
        queries_ref[b] = queries


def projections(block_len, context, question, gain, wq, wk, wv, tables):
    return pl.pallas_call(
        projection_kernel,
        in_specs=[smem, anywhere, anywhere, vmem] + [anywhere] * 5 + [vmem] * 2,
        out_specs=[vmem] * 3,
        out_shape=[
            jax.ShapeDtypeStruct((HEADS, BLK, HD), bf16),
            jax.ShapeDtypeStruct((BLK + QPAD, 2 * HD), bf16),
            jax.ShapeDtypeStruct((N_BLK, QROWS, HEADS * HD), bf16),
        ],
        scratch_shapes=[
            pltpu.VMEM((BLK, HD), f32),
            pltpu.VMEM((BLK, HD), f32),
            pltpu.SemaphoreType.DMA((2,)),
            pltpu.VMEM((BLK, D), bf16),
            pltpu.VMEM((QROWS, D), bf16),
            pltpu.VMEM((D, HEADS * HD), bf16),
            pltpu.VMEM((D, HD), bf16),
            pltpu.VMEM((D, HD), bf16),
            pltpu.VMEM((BLK + QPAD, KC), bf16),
            pltpu.VMEM((BLK + QPAD, (HEADS + 2) * HD), f32),
            pltpu.VMEM((BLK + QPAD, HD), f32),
            pltpu.SemaphoreType.DMA((D // KC, 4)),
            pltpu.SemaphoreType.DMA,
        ],
        compiler_params=params(60),
        cost_estimate=cost(2 * BLK * D * 768, 12 * 2**20),
        name="projections",
    )(block_len, context, question, gain, wq, wk, wv, *tables)


def question_attention_kernel(len_ref, queries_ref, kv_ref, out_ref, token_ref):
    token_ref[...] = jnp.zeros_like(token_ref)
    blk_at = lax.axis_index("blk")
    live = lax.broadcasted_iota(jnp.int32, (QN, BLK), 1) < len_ref[blk_at]
    question_id = lax.broadcasted_iota(jnp.int32, (QN, HD), 0)
    lane = lax.broadcasted_iota(jnp.int32, (QN, HD), 1)
    seen = (lane < QROWS) & (lane + blk_at * QROWS <= question_id)
    own = jnp.concatenate([kv_ref[BLK:], jnp.zeros((HD - QPAD, 2 * HD), bf16)], 0)
    keys = kv_ref[:BLK, :HD]
    values = with_ones(kv_ref[:BLK, HD:])
    own_values = with_ones(own[:, HD:])
    tile = jnp.zeros((QN, HD), f32)
    for h in range(HEADS):
        cols = slice(h * HD, (h + 1) * HD)
        q = queries_ref[:, :, cols].reshape(QN, HD)
        scores = jnp.where(live, dot_t(q, keys), masked_score)
        own_scores = jnp.where(seen, dot_t(q, own[:, :HD]), masked_score)
        highest = jnp.maximum(
            jnp.max(scores, axis=-1, keepdims=True), jnp.max(own_scores, axis=-1, keepdims=True)
        )
        mixture = dot(jnp.exp2(scores - highest).astype(bf16), values)
        mixture = mixture + dot(jnp.exp2(own_scores - highest).astype(bf16), own_values)
        totals = mixture[:, HD:]
        out_ref[:, :, cols] = (mixture[:, :HD] / totals).reshape(N_BLK, QROWS, HD)
        lse = highest + jnp.log(totals) * log2_e
        tile = jnp.where(lane // 32 == h, lse, tile)
    out_ref[:, :, HEADS * HD :] = tile.reshape(N_BLK, QROWS, HD)


def question_attention(block_len, queries, kv):
    return pl.pallas_call(
        question_attention_kernel,
        out_shape=[
            jax.ShapeDtypeStruct((N_BLK, QROWS, (HEADS + 1) * HD), f32),
            jax.ShapeDtypeStruct((8, HD), f32),
        ],
        in_specs=[smem] + [vmem] * 2,
        out_specs=[vmem] * 2,
        compiler_params=params(),
        cost_estimate=cost(HEADS * QN * 640 * HD * 8, 2**20, HEADS * QN * 640),
        name="question_attention",
    )(block_len, queries, kv)


def merged(qlen_ref, parts_ref):
    row = lax.broadcasted_iota(jnp.int32, (QROWS, HD), 0) + lax.axis_index("blk") * QROWS
    valid = row < qlen_ref[0]
    heads = []
    for h in range(HEADS):
        lse = parts_ref[:, :, HEADS * HD + h * 32 : HEADS * HD + h * 32 + 1]
        top = jnp.max(lse, axis=0, keepdims=True)
        share = jnp.exp2(lse - top)
        mixture = jnp.sum(parts_ref[:, :, h * HD : (h + 1) * HD] * share, axis=0)
        heads.append(jnp.where(valid, mixture / jnp.sum(share, axis=0), 0.0))
    rows = jnp.concatenate(heads, axis=1)
    return jnp.concatenate([rows, jnp.zeros((QPAD - QROWS, HEADS * HD), f32)], 0).astype(bf16)


def context_kernel(
    len_ref, q_ref, kv_ref, akv_ref, w_hbm, _, *refs
):
    keep_refs, send_refs, (att_ref, w_ref, sem) = refs[:NY], refs[NY : 2 * NY], refs[2 * NY :]
    blk_at, kv_at = lax.axis_index("blk"), lax.axis_index("kv")
    y_at, c_at = kv_at // NC, lax.rem(kv_at, NC)
    copy = pltpu.make_async_copy(w_hbm, w_ref, sem)
    copy.start()
    first = blk_at == 0
    row = lax.broadcasted_iota(jnp.int32, (ROWS, ROWS), 0)
    causal = lax.broadcasted_iota(jnp.int32, (ROWS, ROWS), 1) <= row
    anchor_keys = akv_ref[:BLK, :HD]
    anchor_values = with_ones(akv_ref[:BLK, HD:])
    values = with_ones(kv_ref[:BLK, HD:])
    for r in range(BLK // ROWS):
        rows, before = slice(r * ROWS, (r + 1) * ROWS), slice(0, r * ROWS)
        valid = lax.broadcasted_iota(jnp.int32, (ROWS, HD), 0) + r * ROWS < len_ref[blk_at]
        for h in range(HEADS):
            q = q_ref[h, rows, :]
            anchor = dot_t(q, anchor_keys)
            own = [jnp.where(causal, dot_t(q, kv_ref[rows, :HD]), masked_score)]
            if r:
                own.append(dot_t(q, kv_ref[before, :HD]))
            highest = jnp.max(own[0], axis=-1, keepdims=True)
            for scores in own[1:]:
                highest = jnp.maximum(highest, jnp.max(scores, axis=-1, keepdims=True))
            anchor_highest = jnp.max(anchor, axis=-1, keepdims=True)
            highest = jnp.where(first, highest, jnp.maximum(highest, anchor_highest))
            weights = jnp.exp2(anchor - jnp.where(first, -masked_score, highest))
            mixture = dot(weights.astype(bf16), anchor_values)
            for scores, at in zip(own, (rows, before)):
                mixture = mixture + dot(jnp.exp2(scores - highest).astype(bf16), values[at])
            result = mixture[:, :HD] / mixture[:, HD:]
            att_ref[rows, h * HD : (h + 1) * HD] = jnp.where(valid, result, 0.0).astype(bf16)
    copy.wait()
    for d in range(NY):
        to_y = lax.rem(y_at + d, NY)
        for ref, to_c in ((send_refs[d], 1 - c_at), (keep_refs[d], c_at)):
            columns = pl.ds(pl.multiple_of((to_y * NC + to_c) * FEAT, FEAT), FEAT)
            ref[...] = dot(att_ref[...], w_ref[:, columns]).astype(bf16)


def context_attention(block_len, q, kv, anchor, w_out, after):
    return pl.pallas_call(
        context_kernel,
        in_specs=[smem] + [vmem] * 3 + [anywhere] * 2,
        out_specs=[vmem] * (2 * NY),
        out_shape=[jax.ShapeDtypeStruct((BLK, FEAT), bf16)] * (2 * NY),
        scratch_shapes=[
            pltpu.VMEM((BLK, HEADS * HD), bf16),
            pltpu.VMEM((HEADS * HD, D), bf16),
            pltpu.SemaphoreType.DMA,
        ],
        compiler_params=params(47),
        cost_estimate=cost(HEADS * BLK * BLK * HD * 8 * 20, 4 * 2**20, HEADS * BLK * BLK),
        name="context_attention",
    )(block_len, q, kv, anchor, w_out, after)


def question_output_kernel(qlen_ref, parts_ref, w_hbm, _, keep_ref, send_ref, w_ref, sem):
    copy = pltpu.make_async_copy(w_hbm, w_ref, sem)
    copy.start()
    kv_at = lax.axis_index("kv")
    y_at, c_at = kv_at // NC, lax.rem(kv_at, NC)
    rows = merged(qlen_ref, parts_ref)
    copy.wait()
    for d in range(NY):
        to_y = lax.rem(y_at + d, NY)
        for ref, to_c in ((send_ref, 1 - c_at), (keep_ref, c_at)):
            columns = pl.ds(pl.multiple_of((to_y * NC + to_c) * FEAT, FEAT), FEAT)
            ref[d] = dot(rows, w_ref[:, columns]).astype(bf16)


def question_output(question_len, parts, w_out, after):
    return pl.pallas_call(
        question_output_kernel,
        in_specs=[smem, vmem] + [anywhere] * 2,
        out_specs=[vmem] * 2,
        out_shape=[jax.ShapeDtypeStruct((NY, QPAD, FEAT), bf16)] * 2,
        scratch_shapes=[pltpu.VMEM((HEADS * HD, D), bf16), pltpu.SemaphoreType.DMA],
        compiler_params=params(56),
        cost_estimate=cost(400 * 256 * HEADS * HD * FEAT * NY, 4 * 2**20),
        name="question_output",
    )(question_len, parts, w_out, after)


def total_of(*parts):
    total = parts[0].astype(f32)
    for part in parts[1:]:
        total = total + part.astype(f32)
    return total.astype(bf16)


def across_kernel(keep_ref, got_ref, first_ref, second_ref):
    first_ref[...] = total_of(keep_ref[:ROWS], got_ref[:ROWS])
    second_ref[...] = total_of(keep_ref[ROWS:], got_ref[ROWS:])


def across_sum(keep, got):
    return pl.pallas_call(
        across_kernel,
        in_specs=[vmem] * 2,
        out_specs=[vmem] * 2,
        out_shape=[jax.ShapeDtypeStruct((ROWS, FEAT), bf16)] * 2,
        compiler_params=params(),
        cost_estimate=cost(0, 0),
        name="across_sum",
    )(keep, got)


def others_kernel(near_keep, near_got, far_keep, far_got, near_a, near_b, far_a, far_b):
    near_a[...] = total_of(near_keep[:ROWS], near_got[:ROWS])
    near_b[...] = total_of(near_keep[ROWS:], near_got[ROWS:])
    far_a[...] = total_of(far_keep[:ROWS], far_got[:ROWS])
    far_b[...] = total_of(far_keep[ROWS:], far_got[ROWS:])


def others_sum(*parts):
    return pl.pallas_call(
        others_kernel,
        in_specs=[vmem] * 4,
        out_specs=[vmem] * 4,
        out_shape=[jax.ShapeDtypeStruct((ROWS, FEAT), bf16)] * 4,
        compiler_params=params(),
        cost_estimate=cost(0, 0),
        name="others_sum",
    )(*parts)


def relay_kernel(
    near_ref, far_ref, first_ref, second_ref, q_keep, q_got, _, __,
    near_out, far_out, q_own_out, q_across_out,
):
    near_out[:ROWS] = total_of(near_ref[...], first_ref[...])
    far_out[:ROWS] = total_of(far_ref[...], second_ref[...])
    for d, out in enumerate((q_own_out, near_out.at[ROWS:], q_across_out, far_out.at[ROWS:])):
        out[...] = total_of(q_keep[d], q_got[d])


def relay(*parts):
    half = jax.ShapeDtypeStruct((ROWS + QPAD, FEAT), bf16)
    return pl.pallas_call(
        relay_kernel,
        in_specs=[vmem] * 6 + [anywhere] * 2,
        out_specs=[vmem] * 4,
        out_shape=[half] * 2 + [jax.ShapeDtypeStruct((QPAD, FEAT), bf16)] * 2,
        compiler_params=params(),
        cost_estimate=cost(BLK * FEAT, BLK * FEAT * 10),
        name="relay",
    )(*parts)


def finish_kernel(
    keep, got, left_a, left_b, right_a, right_b, q_own, q_across, out_ref, question_ref
):
    out_ref[:ROWS] = total_of(keep[:ROWS], got[:ROWS], left_a[:ROWS], right_a[...])
    out_ref[ROWS:] = total_of(keep[ROWS:], got[ROWS:], left_b[...], right_b[:ROWS])
    question = total_of(q_own[...], left_a[ROWS:], right_b[ROWS:], q_across[...])
    question_ref[...] = question[:QROWS]


def finish(*parts):
    return pl.pallas_call(
        finish_kernel,
        in_specs=[vmem] * len(parts),
        out_specs=[vmem] * 2,
        out_shape=[
            jax.ShapeDtypeStruct((BLK, FEAT), bf16),
            jax.ShapeDtypeStruct((QROWS, FEAT), bf16),
        ],
        compiler_params=params(),
        cost_estimate=cost(BLK * FEAT * 4, BLK * FEAT * 10),
        name="finish",
    )(*parts)


def sum_kernel(*refs):
    total = refs[0][...].astype(f32)
    for ref in refs[1:-2]:
        total = total + ref[...].astype(f32)
    refs[-1][...] = total.astype(bf16)


def sum_of(*parts, after):
    return pl.pallas_call(
        sum_kernel,
        in_specs=[vmem] * len(parts) + [anywhere],
        out_specs=vmem,
        out_shape=jax.ShapeDtypeStruct(parts[0].shape, bf16),
        compiler_params=params(),
        cost_estimate=cost(BLK * 256 * 3, BLK * 256 * 8),
        name="sum_of",
    )(*parts, after)


def to_blocks(pairs):
    return [(a * NZ + b, c * NZ + d) for (a, b), (c, d) in pairs.items()]


def shift_y(value, by):
    pairs = [(y * NC + c, (y + by) % NY * NC + c) for y in range(NY) for c in range(NC)]
    return lax.ppermute(value, "kv", pairs)


def swap_cores(value):
    pairs = [(y * NC + c, y * NC + 1 - c) for y in range(NY) for c in range(NC)]
    return lax.ppermute(value, "kv", pairs)


def body(context, question, norm_gain, w_query, w_key, w_value, w_out, block_len, question_len):
    blk_at = lax.axis_index("blk")
    tables = [jnp.asarray(t) for t in angle_tables(np.arange(BLK))]
    tables += [jnp.asarray(t) for t in angle_tables(np.arange(N_BLK + 1) * BLK)]

    q, kv, queries = projections(
        block_len, context, question, norm_gain.reshape(1, D), w_query, w_key, w_value, tables
    )
    held = jnp.where(blk_at == 0, kv, jnp.zeros_like(kv))
    held = held + lax.ppermute(kv, "blk", to_blocks({(0, 0): (2, 0)}))
    held = held + lax.ppermute(kv, "blk", to_blocks({(0, 0): (0, 3)}))
    held = held + lax.ppermute(kv, "blk", to_blocks({(0, 0): (0, 5)}))
    queries = lax.all_to_all(queries, "blk", 0, 0)
    within = {(0, 0): (0, 1), (0, 3): (0, 4), (0, 5): (0, 6)}, {(0, 0): (0, 7), (0, 3): (0, 2)}
    second = lax.ppermute(held, "blk", to_blocks({**within[0], (2, 0): (2, 3)}))
    third = lax.ppermute(held, "blk", to_blocks({**within[1], (2, 0): (2, 5)}))
    parts, token = question_attention(block_len, queries, kv)
    held = sum_of(held, second, third, after=token)
    anchor = held
    for x, pairs in zip((1, 3), within):
        pairs = {(2, a): (2, b) for (_, a), (_, b) in pairs.items()}
        across = {(0, z): (x, z) for z in range(NZ)}
        anchor = anchor + lax.ppermute(held, "blk", to_blocks({**across, **pairs}))
    parts = lax.all_to_all(parts, "blk", 0, 0)

    products = context_attention(block_len, q, kv, anchor, w_out, token)
    keep, send = products[:NY], products[NY:]
    first, second = across_sum(keep[2], swap_cores(send[2]))
    near_a, near_b, far_a, far_b = others_sum(
        keep[1], swap_cores(send[1]), keep[3], swap_cores(send[3])
    )
    left_b, right_a = shift_y(near_b, 1), shift_y(far_a, 3)
    q_keep, q_send = question_output(question_len, parts, w_out, first)
    first, second = shift_y(first, 1), shift_y(second, 3)
    near, far, q_own, q_across = relay(
        near_a, far_b, first, second, q_keep, swap_cores(q_send), left_b, right_a
    )
    left_a, right_b = shift_y(near, 1), shift_y(far, 3)
    q_across = shift_y(q_across, 2)
    own = keep[0], swap_cores(send[0])
    return finish(*own, left_a, left_b, right_a, right_b, q_own, q_across)


def solution(mesh):
    return jax.shard_map(
        body,
        mesh=mesh,
        in_specs=(
            P("blk", None),
            P("blk", None),
            P(),
            P(None, "kv"),
            P(None, "kv"),
            P(None, "kv"),
            P("kv", None),
            P(),
            P(),
        ),
        out_specs=(P("blk", "kv"), P("blk", "kv")),
        check_vma=False,
    )
```

```python
import functools

import jax
import jax.numpy as jnp
import numpy as np
from jax import lax
from jax.experimental import pallas as pl
from jax.experimental.pallas import tpu as pltpu
from jax.sharding import PartitionSpec as P

HD = 128
HEADS = 4
BLK = 512
QROWS = 8
NX, NZ, NY, NC = 4, 8, 4, 2
N_BLK, N_KV = NX * NZ, NY * NC
QN = N_BLK * QROWS
D = 4096
FEAT = D // N_KV
KC = 1024
ROWS = 256
QPAD = 16

epsilon = 1e-05
rope_base = 500000.0
masked_score = -1e30
q_scale = float(HD**-0.5 * np.log2(np.e))
log2_e = float(np.log2(np.e))

bf16 = jnp.bfloat16
f32 = jnp.float32


def angle_tables(positions):
    inverse_freq = rope_base ** (-2.0 * np.arange(HD // 2, dtype=np.float64) / HD)
    angles = np.asarray(positions, np.float64)[:, None] * inverse_freq[None, :]
    angles = np.concatenate([angles, angles], 1)
    return np.cos(angles).astype(np.float32), np.sin(angles).astype(np.float32)


def params(limit=24):
    return pltpu.CompilerParams(vmem_limit_bytes=limit * 2**20)


def cost(flops, bytes_accessed, transcendentals=0):
    return pl.CostEstimate(
        flops=flops, bytes_accessed=bytes_accessed, transcendentals=transcendentals
    )


def add_angles(first, second):
    return (
        first[0] * second[0] - first[1] * second[1],
        first[1] * second[0] + first[0] * second[1],
    )


def rotated(head, cosine, sine_signed):
    return head * cosine + pltpu.roll(head, HD // 2, 1) * sine_signed


def signed(sine):
    lane = lax.broadcasted_iota(jnp.int32, sine.shape, 1)
    return jnp.where(lane < HD // 2, -sine, sine)


def dot(a, b):
    return jnp.dot(a, b, preferred_element_type=f32)


def dot_t(a, b):
    return lax.dot_general(a, b, (((1,), (1,)), ((), ())), preferred_element_type=f32)


def lane_folded(values):
    total = values[:, :HD]
    for part in range(1, values.shape[1] // HD):
        total = total + values[:, part * HD : (part + 1) * HD]
    return total


def squares_to_factor(squares):
    mean = jnp.sum(squares, axis=-1, keepdims=True) * (1.0 / D)
    return lax.rsqrt(mean + epsilon)


smem = pl.BlockSpec(memory_space=pltpu.SMEM)
vmem = pl.BlockSpec(memory_space=pltpu.VMEM)
anywhere = pl.BlockSpec(memory_space=pl.ANY)


def with_ones(values):
    return jnp.concatenate([values, jnp.ones_like(values)], axis=1)


def projection_kernel(
    len_ref, x_hbm, question_hbm, gain_ref, wq_hbm, wk_hbm, wv_hbm, ct_hbm, st_hbm, cb_ref, sb_ref,
    q_ref, kv_ref, queries_ref, ct_ref, st_ref, table_sems,
    x_ref, question_ref, wq_ref, wk_ref, wv_ref, scaled_ref, acc_ref, sq_ref, sems, question_sem,
):
    blk_at = lax.axis_index("blk")
    steps = D // KC
    width = HEADS * HD

    def copies(k):
        part = pl.ds(pl.multiple_of(k * KC, KC), KC)
        return [
            pltpu.make_async_copy(x_hbm.at[:, part], x_ref.at[:, part], sems.at[k, 0]),
            pltpu.make_async_copy(wq_hbm.at[part, :], wq_ref.at[part, :], sems.at[k, 1]),
            pltpu.make_async_copy(wk_hbm.at[part, :], wk_ref.at[part, :], sems.at[k, 2]),
            pltpu.make_async_copy(wv_hbm.at[part, :], wv_ref.at[part, :], sems.at[k, 3]),
        ]

    question_copy = pltpu.make_async_copy(question_hbm, question_ref, question_sem)
    question_copy.start()
    for k in range(2):
        for copy in copies(k):
            copy.start()
    table_copies = [
        pltpu.make_async_copy(ct_hbm, ct_ref, table_sems.at[0]),
        pltpu.make_async_copy(st_hbm, st_ref, table_sems.at[1]),
    ]
    for copy in table_copies:
        copy.start()
    acc_ref[...] = jnp.zeros_like(acc_ref)
    sq_ref[...] = jnp.zeros_like(sq_ref)
    question_copy.wait()

    def turn(k, _):
        for copy in copies(k):
            copy.wait()

        @pl.when(k + 2 < steps)
        def _():
            for copy in copies(k + 2):
                copy.start()

        part = pl.ds(pl.multiple_of(k * KC, KC), KC)
        gain = gain_ref[:, part]
        x = x_ref[:, part].astype(f32)
        sq_ref[:BLK] += lane_folded(x * x)
        scaled_ref[:BLK] = (x * gain).astype(bf16)
        x = question_ref[:, part].astype(f32)
        x = jnp.concatenate([x, jnp.zeros((QPAD - QROWS, KC), f32)], 0)
        sq_ref[BLK:] += lane_folded(x * x)
        scaled_ref[BLK:] = (x * gain).astype(bf16)
        acc_ref[:, :width] += dot(scaled_ref[...], wq_ref[part, :])
        acc_ref[:, width:] += dot(scaled_ref[...], jnp.concatenate([wk_ref[part, :], wv_ref[part, :]], axis=1))
        return 0

    lax.fori_loop(0, steps, turn, 0)
    for copy in table_copies:
        copy.wait()

    factor = squares_to_factor(sq_ref[...])
    block = pl.ds(blk_at, 1)
    tokens = (ct_ref[...], st_ref[...])
    cosine, sine = add_angles(tokens, (cb_ref[block, :], sb_ref[block, :]))
    total = len_ref[0]
    for b in range(1, N_BLK):
        total = total + len_ref[b]
    high, low = pl.ds(total // BLK, 1), pl.ds(lax.rem(total, BLK), 1)
    base = add_angles((cb_ref[high, :], sb_ref[high, :]), (ct_ref[low, :], st_ref[low, :]))
    rows = pl.ds(pl.multiple_of(blk_at * QROWS, QROWS), QROWS)
    own_cosine, own_sine = add_angles((ct_ref[rows, :], st_ref[rows, :]), base)

    def heads_of(rows, cosine, sine):
        scale = factor[rows]
        cosine, sine = cosine * scale, signed(sine) * scale
        heads = [acc_ref[rows, h * HD : (h + 1) * HD] for h in range(HEADS + 2)]
        turned = [rotated(head, cosine, sine) for head in heads[: HEADS + 1]]
        return [head * q_scale for head in turned[:HEADS]], turned[HEADS], heads[HEADS + 1] * scale

    queries, key, value = heads_of(slice(0, BLK), cosine, sine)
    for h in range(HEADS):
        q_ref[h] = queries[h].astype(bf16)
    kv_ref[:BLK, :HD] = key.astype(bf16)
    kv_ref[:BLK, HD:] = value.astype(bf16)
    queries, key, value = heads_of(slice(BLK, BLK + QROWS), own_cosine, own_sine)
    own = jnp.concatenate([key, value], axis=1)
    own = jnp.concatenate([own, jnp.zeros((QPAD - QROWS, 2 * HD), f32)], axis=0)
    kv_ref[BLK:] = own.astype(bf16)
    queries = jnp.concatenate(queries, axis=1).astype(bf16)
    for b in range(N_BLK):
        queries_ref[b] = queries


def projections(block_len, context, question, gain, wq, wk, wv, tables):
    return pl.pallas_call(
        projection_kernel,
        in_specs=[smem, anywhere, anywhere, vmem] + [anywhere] * 5 + [vmem] * 2,
        out_specs=[vmem] * 3,
        out_shape=[
            jax.ShapeDtypeStruct((HEADS, BLK, HD), bf16),
            jax.ShapeDtypeStruct((BLK + QPAD, 2 * HD), bf16),
            jax.ShapeDtypeStruct((N_BLK, QROWS, HEADS * HD), bf16),
        ],
        scratch_shapes=[
            pltpu.VMEM((BLK, HD), f32),
            pltpu.VMEM((BLK, HD), f32),
            pltpu.SemaphoreType.DMA((2,)),
            pltpu.VMEM((BLK, D), bf16),
            pltpu.VMEM((QROWS, D), bf16),
            pltpu.VMEM((D, HEADS * HD), bf16),
            pltpu.VMEM((D, HD), bf16),
            pltpu.VMEM((D, HD), bf16),
            pltpu.VMEM((BLK + QPAD, KC), bf16),
            pltpu.VMEM((BLK + QPAD, (HEADS + 2) * HD), f32),
            pltpu.VMEM((BLK + QPAD, HD), f32),
            pltpu.SemaphoreType.DMA((D // KC, 4)),
            pltpu.SemaphoreType.DMA,
        ],
        compiler_params=params(60),
        cost_estimate=cost(2 * BLK * D * 768, 12 * 2**20),
        name="projections",
    )(block_len, context, question, gain, wq, wk, wv, *tables)


def question_attention_kernel(len_ref, queries_ref, kv_ref, out_ref, token_ref):
    token_ref[...] = jnp.zeros_like(token_ref)
    blk_at = lax.axis_index("blk")
    live = lax.broadcasted_iota(jnp.int32, (QN, BLK), 1) < len_ref[blk_at]
    question_id = lax.broadcasted_iota(jnp.int32, (QN, HD), 0)
    lane = lax.broadcasted_iota(jnp.int32, (QN, HD), 1)
    seen = (lane < QROWS) & (lane + blk_at * QROWS <= question_id)
    own = jnp.concatenate([kv_ref[BLK:], jnp.zeros((HD - QPAD, 2 * HD), bf16)], 0)
    keys = kv_ref[:BLK, :HD]
    values = with_ones(kv_ref[:BLK, HD:])
    own_values = with_ones(own[:, HD:])
    tile = jnp.zeros((QN, HD), f32)
    for h in range(HEADS):
        cols = slice(h * HD, (h + 1) * HD)
        q = queries_ref[:, :, cols].reshape(QN, HD)
        scores = jnp.where(live, dot_t(q, keys), masked_score)
        own_scores = jnp.where(seen, dot_t(q, own[:, :HD]), masked_score)
        highest = jnp.maximum(
            jnp.max(scores, axis=-1, keepdims=True), jnp.max(own_scores, axis=-1, keepdims=True)
        )
        mixture = dot(jnp.exp2(scores - highest).astype(bf16), values)
        mixture = mixture + dot(jnp.exp2(own_scores - highest).astype(bf16), own_values)
        totals = mixture[:, HD:]
        out_ref[:, :, cols] = (mixture[:, :HD] / totals).reshape(N_BLK, QROWS, HD)
        lse = highest + jnp.log(totals) * log2_e
        tile = jnp.where(lane // 32 == h, lse, tile)
    out_ref[:, :, HEADS * HD :] = tile.reshape(N_BLK, QROWS, HD)


def question_attention(block_len, queries, kv):
    return pl.pallas_call(
        question_attention_kernel,
        out_shape=[
            jax.ShapeDtypeStruct((N_BLK, QROWS, (HEADS + 1) * HD), f32),
            jax.ShapeDtypeStruct((8, HD), f32),
        ],
        in_specs=[smem] + [vmem] * 2,
        out_specs=[vmem] * 2,
        compiler_params=params(),
        cost_estimate=cost(HEADS * QN * 640 * HD * 8, 2**20, HEADS * QN * 640),
        name="question_attention",
    )(block_len, queries, kv)


def merged(qlen_ref, parts_ref):
    row = lax.broadcasted_iota(jnp.int32, (QROWS, HD), 0) + lax.axis_index("blk") * QROWS
    valid = row < qlen_ref[0]
    heads = []
    for h in range(HEADS):
        lse = parts_ref[:, :, HEADS * HD + h * 32 : HEADS * HD + h * 32 + 1]
        top = jnp.max(lse, axis=0, keepdims=True)
        share = jnp.exp2(lse - top)
        mixture = jnp.sum(parts_ref[:, :, h * HD : (h + 1) * HD] * share, axis=0)
        heads.append(jnp.where(valid, mixture / jnp.sum(share, axis=0), 0.0))
    rows = jnp.concatenate(heads, axis=1)
    return jnp.concatenate([rows, jnp.zeros((QPAD - QROWS, HEADS * HD), f32)], 0).astype(bf16)


def chip_columns(to_y):
    width = NC * FEAT
    return pl.ds(pl.multiple_of(lax.rem(to_y, NY) * width, width), width)


def context_kernel(
    len_ref, q_ref, kv_ref, akv_ref, w_hbm, _, *refs
):
    keep_refs, send_refs, (att_ref, w_ref, sems) = refs[:NY], refs[NY : 2 * NY], refs[2 * NY :]
    blk_at, kv_at = lax.axis_index("blk"), lax.axis_index("kv")
    y_at, c_at = kv_at // NC, lax.rem(kv_at, NC)
    shares = []
    for i, d in enumerate((2, 1, 3, 0)):
        columns = chip_columns(y_at + d)
        copy = pltpu.make_async_copy(w_hbm.at[:, columns], w_ref.at[i], sems.at[i])
        copy.start()
        shares.append((d, copy))
    first = blk_at == 0
    row = lax.broadcasted_iota(jnp.int32, (ROWS, ROWS), 0)
    causal = lax.broadcasted_iota(jnp.int32, (ROWS, ROWS), 1) <= row
    anchor_keys = akv_ref[:BLK, :HD]
    anchor_values = with_ones(akv_ref[:BLK, HD:])
    values = with_ones(kv_ref[:BLK, HD:])
    for r in range(BLK // ROWS):
        rows, before = slice(r * ROWS, (r + 1) * ROWS), slice(0, r * ROWS)
        valid = lax.broadcasted_iota(jnp.int32, (ROWS, HD), 0) + r * ROWS < len_ref[blk_at]
        for h in range(HEADS):
            q = q_ref[h, rows, :]
            anchor = dot_t(q, anchor_keys)
            own = [jnp.where(causal, dot_t(q, kv_ref[rows, :HD]), masked_score)]
            if r:
                own.append(dot_t(q, kv_ref[before, :HD]))
            highest = jnp.max(own[0], axis=-1, keepdims=True)
            for scores in own[1:]:
                highest = jnp.maximum(highest, jnp.max(scores, axis=-1, keepdims=True))
            anchor_highest = jnp.max(anchor, axis=-1, keepdims=True)
            highest = jnp.where(first, highest, jnp.maximum(highest, anchor_highest))
            weights = jnp.exp2(anchor - jnp.where(first, -masked_score, highest))
            mixture = dot(weights.astype(bf16), anchor_values)
            for scores, at in zip(own, (rows, before)):
                mixture = mixture + dot(jnp.exp2(scores - highest).astype(bf16), values[at])
            result = mixture[:, :HD] / mixture[:, HD:]
            att_ref[rows, h * HD : (h + 1) * HD] = jnp.where(valid, result, 0.0).astype(bf16)
    for i, (d, copy) in enumerate(shares):
        copy.wait()
        for ref, to_c in ((send_refs[d], 1 - c_at), (keep_refs[d], c_at)):
            columns = pl.ds(pl.multiple_of(to_c * FEAT, FEAT), FEAT)
            ref[...] = dot(att_ref[...], w_ref[i, :, columns]).astype(bf16)


def context_attention(block_len, q, kv, anchor, w_out, after):
    return pl.pallas_call(
        context_kernel,
        in_specs=[smem] + [vmem] * 3 + [anywhere] * 2,
        out_specs=[vmem] * (2 * NY),
        out_shape=[jax.ShapeDtypeStruct((BLK, FEAT), bf16)] * (2 * NY),
        scratch_shapes=[
            pltpu.VMEM((BLK, HEADS * HD), bf16),
            pltpu.VMEM((NY, HEADS * HD, NC * FEAT), bf16),
            pltpu.SemaphoreType.DMA((NY,)),
        ],
        compiler_params=params(47),
        cost_estimate=cost(HEADS * BLK * BLK * HD * 8 * 20, 4 * 2**20, HEADS * BLK * BLK),
        name="context_attention",
    )(block_len, q, kv, anchor, w_out, after)


def question_output_kernel(qlen_ref, parts_ref, w_hbm, _, keep_ref, send_ref, w_ref, sem):
    copy = pltpu.make_async_copy(w_hbm, w_ref, sem)
    copy.start()
    kv_at = lax.axis_index("kv")
    y_at, c_at = kv_at // NC, lax.rem(kv_at, NC)
    rows = merged(qlen_ref, parts_ref)
    copy.wait()
    for d in range(NY):
        to_y = lax.rem(y_at + d, NY)
        for ref, to_c in ((send_ref, 1 - c_at), (keep_ref, c_at)):
            columns = pl.ds(pl.multiple_of((to_y * NC + to_c) * FEAT, FEAT), FEAT)
            ref[d] = dot(rows, w_ref[:, columns]).astype(bf16)


def question_output(question_len, parts, w_out, after):
    return pl.pallas_call(
        question_output_kernel,
        in_specs=[smem, vmem] + [anywhere] * 2,
        out_specs=[vmem] * 2,
        out_shape=[jax.ShapeDtypeStruct((NY, QPAD, FEAT), bf16)] * 2,
        scratch_shapes=[pltpu.VMEM((HEADS * HD, D), bf16), pltpu.SemaphoreType.DMA],
        compiler_params=params(56),
        cost_estimate=cost(400 * 256 * HEADS * HD * FEAT * NY, 4 * 2**20),
        name="question_output",
    )(question_len, parts, w_out, after)


def total_of(*parts):
    total = parts[0].astype(f32)
    for part in parts[1:]:
        total = total + part.astype(f32)
    return total.astype(bf16)


def across_kernel(keep_ref, got_ref, first_ref, second_ref):
    first_ref[...] = total_of(keep_ref[:ROWS], got_ref[:ROWS])
    second_ref[...] = total_of(keep_ref[ROWS:], got_ref[ROWS:])


def across_sum(keep, got):
    return pl.pallas_call(
        across_kernel,
        in_specs=[vmem] * 2,
        out_specs=[vmem] * 2,
        out_shape=[jax.ShapeDtypeStruct((ROWS, FEAT), bf16)] * 2,
        compiler_params=params(),
        cost_estimate=cost(0, 0),
        name="across_sum",
    )(keep, got)


def others_kernel(near_keep, near_got, far_keep, far_got, near_a, near_b, far_a, far_b):
    near_a[...] = total_of(near_keep[:ROWS], near_got[:ROWS])
    near_b[...] = total_of(near_keep[ROWS:], near_got[ROWS:])
    far_a[...] = total_of(far_keep[:ROWS], far_got[:ROWS])
    far_b[...] = total_of(far_keep[ROWS:], far_got[ROWS:])


def others_sum(*parts):
    return pl.pallas_call(
        others_kernel,
        in_specs=[vmem] * 4,
        out_specs=[vmem] * 4,
        out_shape=[jax.ShapeDtypeStruct((ROWS, FEAT), bf16)] * 4,
        compiler_params=params(),
        cost_estimate=cost(0, 0),
        name="others_sum",
    )(*parts)


def relay_kernel(
    near_ref, far_ref, first_ref, second_ref, q_keep, q_got, _, __,
    near_out, far_out, q_own_out, q_across_out,
):
    near_out[:ROWS] = total_of(near_ref[...], first_ref[...])
    far_out[:ROWS] = total_of(far_ref[...], second_ref[...])
    for d, out in enumerate((q_own_out, near_out.at[ROWS:], q_across_out, far_out.at[ROWS:])):
        out[...] = total_of(q_keep[d], q_got[d])


def relay(*parts):
    half = jax.ShapeDtypeStruct((ROWS + QPAD, FEAT), bf16)
    return pl.pallas_call(
        relay_kernel,
        in_specs=[vmem] * 6 + [anywhere] * 2,
        out_specs=[vmem] * 4,
        out_shape=[half] * 2 + [jax.ShapeDtypeStruct((QPAD, FEAT), bf16)] * 2,
        compiler_params=params(),
        cost_estimate=cost(BLK * FEAT, BLK * FEAT * 10),
        name="relay",
    )(*parts)


def finish_kernel(
    keep, got, left_a, left_b, right_a, right_b, q_own, q_across, out_ref, question_ref
):
    out_ref[:ROWS] = total_of(keep[:ROWS], got[:ROWS], left_a[:ROWS], right_a[...])
    out_ref[ROWS:] = total_of(keep[ROWS:], got[ROWS:], left_b[...], right_b[:ROWS])
    question = total_of(q_own[...], left_a[ROWS:], right_b[ROWS:], q_across[...])
    question_ref[...] = question[:QROWS]


def finish(*parts):
    return pl.pallas_call(
        finish_kernel,
        in_specs=[vmem] * len(parts),
        out_specs=[vmem] * 2,
        out_shape=[
            jax.ShapeDtypeStruct((BLK, FEAT), bf16),
            jax.ShapeDtypeStruct((QROWS, FEAT), bf16),
        ],
        compiler_params=params(),
        cost_estimate=cost(BLK * FEAT * 4, BLK * FEAT * 10),
        name="finish",
    )(*parts)


def sum_kernel(*refs):
    total = refs[0][...].astype(f32)
    for ref in refs[1:-2]:
        total = total + ref[...].astype(f32)
    refs[-1][...] = total.astype(bf16)


def sum_of(*parts, after):
    return pl.pallas_call(
        sum_kernel,
        in_specs=[vmem] * len(parts) + [anywhere],
        out_specs=vmem,
        out_shape=jax.ShapeDtypeStruct(parts[0].shape, bf16),
        compiler_params=params(),
        cost_estimate=cost(BLK * 256 * 3, BLK * 256 * 8),
        name="sum_of",
    )(*parts, after)


def to_blocks(pairs):
    return [(a * NZ + b, c * NZ + d) for (a, b), (c, d) in pairs.items()]


def shift_y(value, by):
    pairs = [(y * NC + c, (y + by) % NY * NC + c) for y in range(NY) for c in range(NC)]
    return lax.ppermute(value, "kv", pairs)


def swap_cores(value):
    pairs = [(y * NC + c, y * NC + 1 - c) for y in range(NY) for c in range(NC)]
    return lax.ppermute(value, "kv", pairs)


def body(context, question, norm_gain, w_query, w_key, w_value, w_out, block_len, question_len):
    blk_at = lax.axis_index("blk")
    tables = [jnp.asarray(t) for t in angle_tables(np.arange(BLK))]
    tables += [jnp.asarray(t) for t in angle_tables(np.arange(N_BLK + 1) * BLK)]

    q, kv, queries = projections(
        block_len, context, question, norm_gain.reshape(1, D), w_query, w_key, w_value, tables
    )
    held = jnp.where(blk_at == 0, kv, jnp.zeros_like(kv))
    held = held + lax.ppermute(kv, "blk", to_blocks({(0, 0): (2, 0)}))
    held = held + lax.ppermute(kv, "blk", to_blocks({(0, 0): (0, 3)}))
    held = held + lax.ppermute(kv, "blk", to_blocks({(0, 0): (0, 5)}))
    queries = lax.all_to_all(queries, "blk", 0, 0)
    within = {(0, 0): (0, 1), (0, 3): (0, 4), (0, 5): (0, 6)}, {(0, 0): (0, 7), (0, 3): (0, 2)}
    second = lax.ppermute(held, "blk", to_blocks({**within[0], (2, 0): (2, 3)}))
    third = lax.ppermute(held, "blk", to_blocks({**within[1], (2, 0): (2, 5)}))
    parts, token = question_attention(block_len, queries, kv)
    held = sum_of(held, second, third, after=token)
    anchor = held
    for x, pairs in zip((1, 3), within):
        pairs = {(2, a): (2, b) for (_, a), (_, b) in pairs.items()}
        across = {(0, z): (x, z) for z in range(NZ)}
        anchor = anchor + lax.ppermute(held, "blk", to_blocks({**across, **pairs}))
    parts = lax.all_to_all(parts, "blk", 0, 0)

    products = context_attention(block_len, q, kv, anchor, w_out, token)
    keep, send = products[:NY], products[NY:]
    first, second = across_sum(keep[2], swap_cores(send[2]))
    near_a, near_b, far_a, far_b = others_sum(
        keep[1], swap_cores(send[1]), keep[3], swap_cores(send[3])
    )
    left_b, right_a = shift_y(near_b, 1), shift_y(far_a, 3)
    q_keep, q_send = question_output(question_len, parts, w_out, first)
    first, second = shift_y(first, 1), shift_y(second, 3)
    near, far, q_own, q_across = relay(
        near_a, far_b, first, second, q_keep, swap_cores(q_send), left_b, right_a
    )
    left_a, right_b = shift_y(near, 1), shift_y(far, 3)
    q_across = shift_y(q_across, 2)
    own = keep[0], swap_cores(send[0])
    return finish(*own, left_a, left_b, right_a, right_b, q_own, q_across)


def solution(mesh):
    return jax.shard_map(
        body,
        mesh=mesh,
        in_specs=(
            P("blk", None),
            P("blk", None),
            P(),
            P(None, "kv"),
            P(None, "kv"),
            P(None, "kv"),
            P("kv", None),
            P(),
            P(),
        ),
        out_specs=(P("blk", "kv"), P("blk", "kv")),
        check_vma=False,
    )
```

```python
import functools

import jax
import jax.numpy as jnp
import numpy as np
from jax import lax
from jax.experimental import pallas as pl
from jax.experimental.pallas import tpu as pltpu
from jax.sharding import PartitionSpec as P

HD = 128
HEADS = 4
BLK = 512
QROWS = 8
NX, NZ, NY, NC = 4, 8, 4, 2
N_BLK, N_KV = NX * NZ, NY * NC
QN = N_BLK * QROWS
D = 4096
FEAT = D // N_KV
KC = 1024
ROWS = 256
QPAD = 16

epsilon = 1e-05
rope_base = 500000.0
masked_score = -1e30
q_scale = float(HD**-0.5 * np.log2(np.e))
log2_e = float(np.log2(np.e))

bf16 = jnp.bfloat16
f32 = jnp.float32


def angle_tables(positions):
    inverse_freq = rope_base ** (-2.0 * np.arange(HD // 2, dtype=np.float64) / HD)
    angles = np.asarray(positions, np.float64)[:, None] * inverse_freq[None, :]
    angles = np.concatenate([angles, angles], 1)
    return np.cos(angles).astype(np.float32), np.sin(angles).astype(np.float32)


def params(limit=24):
    return pltpu.CompilerParams(vmem_limit_bytes=limit * 2**20)


def cost(flops, bytes_accessed, transcendentals=0):
    return pl.CostEstimate(
        flops=flops, bytes_accessed=bytes_accessed, transcendentals=transcendentals
    )


def add_angles(first, second):
    return (
        first[0] * second[0] - first[1] * second[1],
        first[1] * second[0] + first[0] * second[1],
    )


def rotated(head, cosine, sine_signed):
    return head * cosine + pltpu.roll(head, HD // 2, 1) * sine_signed


def signed(sine):
    lane = lax.broadcasted_iota(jnp.int32, sine.shape, 1)
    return jnp.where(lane < HD // 2, -sine, sine)


def dot(a, b):
    return jnp.dot(a, b, preferred_element_type=f32)


def dot_t(a, b):
    return lax.dot_general(a, b, (((1,), (1,)), ((), ())), preferred_element_type=f32)


def lane_folded(values):
    total = values[:, :HD]
    for part in range(1, values.shape[1] // HD):
        total = total + values[:, part * HD : (part + 1) * HD]
    return total


def squares_to_factor(squares):
    mean = jnp.sum(squares, axis=-1, keepdims=True) * (1.0 / D)
    return lax.rsqrt(mean + epsilon)


smem = pl.BlockSpec(memory_space=pltpu.SMEM)
vmem = pl.BlockSpec(memory_space=pltpu.VMEM)
anywhere = pl.BlockSpec(memory_space=pl.ANY)


def with_ones(values):
    return jnp.concatenate([values, jnp.ones_like(values)], axis=1)


def projection_kernel(
    len_ref, x_hbm, question_hbm, gain_ref, wq_hbm, wk_hbm, wv_hbm, ct_hbm, st_hbm, cb_ref, sb_ref,
    q_ref, kv_ref, queries_ref, ct_ref, st_ref, table_sems,
    x_ref, question_ref, wq_ref, wk_ref, wv_ref, scaled_ref, acc_ref, sq_ref, sems, question_sem,
):
    blk_at = lax.axis_index("blk")
    steps = D // KC
    width = HEADS * HD

    def copies(k):
        part = pl.ds(pl.multiple_of(k * KC, KC), KC)
        return [
            pltpu.make_async_copy(x_hbm.at[:, part], x_ref.at[:, part], sems.at[k, 0]),
            pltpu.make_async_copy(wq_hbm.at[part, :], wq_ref.at[part, :], sems.at[k, 1]),
            pltpu.make_async_copy(wk_hbm.at[part, :], wk_ref.at[part, :], sems.at[k, 2]),
            pltpu.make_async_copy(wv_hbm.at[part, :], wv_ref.at[part, :], sems.at[k, 3]),
        ]

    question_copy = pltpu.make_async_copy(question_hbm, question_ref, question_sem)
    question_copy.start()
    for k in range(2):
        for copy in copies(k):
            copy.start()
    table_copies = [
        pltpu.make_async_copy(ct_hbm, ct_ref, table_sems.at[0]),
        pltpu.make_async_copy(st_hbm, st_ref, table_sems.at[1]),
    ]
    for copy in table_copies:
        copy.start()
    acc_ref[...] = jnp.zeros_like(acc_ref)
    sq_ref[...] = jnp.zeros_like(sq_ref)
    question_copy.wait()

    def turn(k, _):
        for copy in copies(k):
            copy.wait()

        @pl.when(k + 2 < steps)
        def _():
            for copy in copies(k + 2):
                copy.start()

        part = pl.ds(pl.multiple_of(k * KC, KC), KC)
        gain = gain_ref[:, part]
        x = x_ref[:, part].astype(f32)
        sq_ref[:BLK] += lane_folded(x * x)
        scaled_ref[:BLK] = (x * gain).astype(bf16)
        x = question_ref[:, part].astype(f32)
        x = jnp.concatenate([x, jnp.zeros((QPAD - QROWS, KC), f32)], 0)
        sq_ref[BLK:] += lane_folded(x * x)
        scaled_ref[BLK:] = (x * gain).astype(bf16)
        acc_ref[:, :width] += dot(scaled_ref[...], wq_ref[part, :])
        acc_ref[:, width:] += dot(scaled_ref[...], jnp.concatenate([wk_ref[part, :], wv_ref[part, :]], axis=1))
        return 0

    lax.fori_loop(0, steps, turn, 0)
    for copy in table_copies:
        copy.wait()

    factor = squares_to_factor(sq_ref[...])
    block = pl.ds(blk_at, 1)
    tokens = (ct_ref[...], st_ref[...])
    cosine, sine = add_angles(tokens, (cb_ref[block, :], sb_ref[block, :]))
    total = len_ref[0]
    for b in range(1, N_BLK):
        total = total + len_ref[b]
    high, low = pl.ds(total // BLK, 1), pl.ds(lax.rem(total, BLK), 1)
    base = add_angles((cb_ref[high, :], sb_ref[high, :]), (ct_ref[low, :], st_ref[low, :]))
    rows = pl.ds(pl.multiple_of(blk_at * QROWS, QROWS), QROWS)
    own_cosine, own_sine = add_angles((ct_ref[rows, :], st_ref[rows, :]), base)

    def heads_of(rows, cosine, sine):
        scale = factor[rows]
        cosine, sine = cosine * scale, signed(sine) * scale
        heads = [acc_ref[rows, h * HD : (h + 1) * HD] for h in range(HEADS + 2)]
        turned = [rotated(head, cosine, sine) for head in heads[: HEADS + 1]]
        return [head * q_scale for head in turned[:HEADS]], turned[HEADS], heads[HEADS + 1] * scale

    queries, key, value = heads_of(slice(0, BLK), cosine, sine)
    for h in range(HEADS):
        q_ref[h] = queries[h].astype(bf16)
    kv_ref[:BLK, :HD] = key.astype(bf16)
    kv_ref[:BLK, HD:] = value.astype(bf16)
    queries, key, value = heads_of(slice(BLK, BLK + QROWS), own_cosine, own_sine)
    own = jnp.concatenate([key, value], axis=1)
    own = jnp.concatenate([own, jnp.zeros((QPAD - QROWS, 2 * HD), f32)], axis=0)
    kv_ref[BLK:] = own.astype(bf16)
    queries = jnp.concatenate(queries, axis=1).astype(bf16)
    for b in range(N_BLK):
        queries_ref[b] = queries


def projections(block_len, context, question, gain, wq, wk, wv, tables):
    return pl.pallas_call(
        projection_kernel,
        in_specs=[smem, anywhere, anywhere, vmem] + [anywhere] * 5 + [vmem] * 2,
        out_specs=[vmem] * 3,
        out_shape=[
            jax.ShapeDtypeStruct((HEADS, BLK, HD), bf16),
            jax.ShapeDtypeStruct((BLK + QPAD, 2 * HD), bf16),
            jax.ShapeDtypeStruct((N_BLK, QROWS, HEADS * HD), bf16),
        ],
        scratch_shapes=[
            pltpu.VMEM((BLK, HD), f32),
            pltpu.VMEM((BLK, HD), f32),
            pltpu.SemaphoreType.DMA((2,)),
            pltpu.VMEM((BLK, D), bf16),
            pltpu.VMEM((QROWS, D), bf16),
            pltpu.VMEM((D, HEADS * HD), bf16),
            pltpu.VMEM((D, HD), bf16),
            pltpu.VMEM((D, HD), bf16),
            pltpu.VMEM((BLK + QPAD, KC), bf16),
            pltpu.VMEM((BLK + QPAD, (HEADS + 2) * HD), f32),
            pltpu.VMEM((BLK + QPAD, HD), f32),
            pltpu.SemaphoreType.DMA((D // KC, 4)),
            pltpu.SemaphoreType.DMA,
        ],
        compiler_params=params(60),
        cost_estimate=cost(2 * BLK * D * 768, 12 * 2**20),
        name="projections",
    )(block_len, context, question, gain, wq, wk, wv, *tables)


def question_attention_kernel(len_ref, queries_ref, kv_ref, out_ref, token_ref):
    token_ref[...] = jnp.zeros_like(token_ref)
    blk_at = lax.axis_index("blk")
    live = lax.broadcasted_iota(jnp.int32, (QN, BLK), 1) < len_ref[blk_at]
    question_id = lax.broadcasted_iota(jnp.int32, (QN, HD), 0)
    lane = lax.broadcasted_iota(jnp.int32, (QN, HD), 1)
    seen = (lane < QROWS) & (lane + blk_at * QROWS <= question_id)
    own = jnp.concatenate([kv_ref[BLK:], jnp.zeros((HD - QPAD, 2 * HD), bf16)], 0)
    keys = kv_ref[:BLK, :HD]
    values = with_ones(kv_ref[:BLK, HD:])
    own_values = with_ones(own[:, HD:])
    tile = jnp.zeros((QN, HD), f32)
    for h in range(HEADS):
        cols = slice(h * HD, (h + 1) * HD)
        q = queries_ref[:, :, cols].reshape(QN, HD)
        scores = jnp.where(live, dot_t(q, keys), masked_score)
        own_scores = jnp.where(seen, dot_t(q, own[:, :HD]), masked_score)
        highest = jnp.maximum(
            jnp.max(scores, axis=-1, keepdims=True), jnp.max(own_scores, axis=-1, keepdims=True)
        )
        mixture = dot(jnp.exp2(scores - highest).astype(bf16), values)
        mixture = mixture + dot(jnp.exp2(own_scores - highest).astype(bf16), own_values)
        totals = mixture[:, HD:]
        out_ref[:, :, cols] = (mixture[:, :HD] / totals).reshape(N_BLK, QROWS, HD)
        lse = highest + jnp.log(totals) * log2_e
        tile = jnp.where(lane // 32 == h, lse, tile)
    out_ref[:, :, HEADS * HD :] = tile.reshape(N_BLK, QROWS, HD)


def question_attention(block_len, queries, kv):
    return pl.pallas_call(
        question_attention_kernel,
        out_shape=[
            jax.ShapeDtypeStruct((N_BLK, QROWS, (HEADS + 1) * HD), f32),
            jax.ShapeDtypeStruct((8, HD), f32),
        ],
        in_specs=[smem] + [vmem] * 2,
        out_specs=[vmem] * 2,
        compiler_params=params(),
        cost_estimate=cost(HEADS * QN * 640 * HD * 8, 2**20, HEADS * QN * 640),
        name="question_attention",
    )(block_len, queries, kv)


def merged(qlen_ref, parts_ref):
    row = lax.broadcasted_iota(jnp.int32, (QROWS, HD), 0) + lax.axis_index("blk") * QROWS
    valid = row < qlen_ref[0]
    heads = []
    for h in range(HEADS):
        lse = parts_ref[:, :, HEADS * HD + h * 32 : HEADS * HD + h * 32 + 1]
        top = jnp.max(lse, axis=0, keepdims=True)
        share = jnp.exp2(lse - top)
        mixture = jnp.sum(parts_ref[:, :, h * HD : (h + 1) * HD] * share, axis=0)
        heads.append(jnp.where(valid, mixture / jnp.sum(share, axis=0), 0.0))
    rows = jnp.concatenate(heads, axis=1)
    return jnp.concatenate([rows, jnp.zeros((QPAD - QROWS, HEADS * HD), f32)], 0).astype(bf16)


def chip_columns(to_y):
    width = NC * FEAT
    return pl.ds(pl.multiple_of(lax.rem(to_y, NY) * width, width), width)


def context_kernel(
    len_ref, q_ref, kv_ref, held_ref, left_ref, right_ref, w_hbm, _, *refs
):
    keep_refs, send_refs, (att_ref, akv_ref, w_ref, sems) = refs[:NY], refs[NY : 2 * NY], refs[2 * NY :]
    akv_ref[...] = held_ref[...] + left_ref[...] + right_ref[...]
    blk_at, kv_at = lax.axis_index("blk"), lax.axis_index("kv")
    y_at, c_at = kv_at // NC, lax.rem(kv_at, NC)
    shares = []
    for i, d in enumerate((2, 1, 3, 0)):
        columns = chip_columns(y_at + d)
        copy = pltpu.make_async_copy(w_hbm.at[:, columns], w_ref.at[i], sems.at[i])
        copy.start()
        shares.append((d, copy))
    first = blk_at == 0
    row = lax.broadcasted_iota(jnp.int32, (ROWS, ROWS), 0)
    causal = lax.broadcasted_iota(jnp.int32, (ROWS, ROWS), 1) <= row
    anchor_keys = akv_ref[:BLK, :HD]
    anchor_values = with_ones(akv_ref[:BLK, HD:])
    values = with_ones(kv_ref[:BLK, HD:])
    for r in range(BLK // ROWS):
        rows, before = slice(r * ROWS, (r + 1) * ROWS), slice(0, r * ROWS)
        valid = lax.broadcasted_iota(jnp.int32, (ROWS, HD), 0) + r * ROWS < len_ref[blk_at]
        for h in range(HEADS):
            q = q_ref[h, rows, :]
            anchor = dot_t(q, anchor_keys)
            own = [jnp.where(causal, dot_t(q, kv_ref[rows, :HD]), masked_score)]
            if r:
                own.append(dot_t(q, kv_ref[before, :HD]))
            highest = jnp.max(own[0], axis=-1, keepdims=True)
            for scores in own[1:]:
                highest = jnp.maximum(highest, jnp.max(scores, axis=-1, keepdims=True))
            anchor_highest = jnp.max(anchor, axis=-1, keepdims=True)
            highest = jnp.where(first, highest, jnp.maximum(highest, anchor_highest))
            weights = jnp.exp2(anchor - jnp.where(first, -masked_score, highest))
            mixture = dot(weights.astype(bf16), anchor_values)
            for scores, at in zip(own, (rows, before)):
                mixture = mixture + dot(jnp.exp2(scores - highest).astype(bf16), values[at])
            result = mixture[:, :HD] / mixture[:, HD:]
            att_ref[rows, h * HD : (h + 1) * HD] = jnp.where(valid, result, 0.0).astype(bf16)
    for i, (d, copy) in enumerate(shares):
        copy.wait()
        for ref, to_c in ((send_refs[d], 1 - c_at), (keep_refs[d], c_at)):
            columns = pl.ds(pl.multiple_of(to_c * FEAT, FEAT), FEAT)
            ref[...] = dot(att_ref[...], w_ref[i, :, columns]).astype(bf16)


def context_attention(block_len, q, kv, anchors, w_out, after):
    return pl.pallas_call(
        context_kernel,
        in_specs=[smem] + [vmem] * 5 + [anywhere] * 2,
        out_specs=[vmem] * (2 * NY),
        out_shape=[jax.ShapeDtypeStruct((BLK, FEAT), bf16)] * (2 * NY),
        scratch_shapes=[
            pltpu.VMEM((BLK, HEADS * HD), bf16),
            pltpu.VMEM((BLK + QPAD, 2 * HD), bf16),
            pltpu.VMEM((NY, HEADS * HD, NC * FEAT), bf16),
            pltpu.SemaphoreType.DMA((NY,)),
        ],
        compiler_params=params(47),
        cost_estimate=cost(HEADS * BLK * BLK * HD * 8 * 20, 4 * 2**20, HEADS * BLK * BLK),
        name="context_attention",
    )(block_len, q, kv, *anchors, w_out, after)


def question_output_kernel(qlen_ref, parts_ref, w_hbm, _, keep_ref, send_ref, w_ref, sem):
    copy = pltpu.make_async_copy(w_hbm, w_ref, sem)
    copy.start()
    kv_at = lax.axis_index("kv")
    y_at, c_at = kv_at // NC, lax.rem(kv_at, NC)
    rows = merged(qlen_ref, parts_ref)
    copy.wait()
    for d in range(NY):
        to_y = lax.rem(y_at + d, NY)
        for ref, to_c in ((send_ref, 1 - c_at), (keep_ref, c_at)):
            columns = pl.ds(pl.multiple_of((to_y * NC + to_c) * FEAT, FEAT), FEAT)
            ref[d] = dot(rows, w_ref[:, columns]).astype(bf16)


def question_output(question_len, parts, w_out, after):
    return pl.pallas_call(
        question_output_kernel,
        in_specs=[smem, vmem] + [anywhere] * 2,
        out_specs=[vmem] * 2,
        out_shape=[jax.ShapeDtypeStruct((NY, QPAD, FEAT), bf16)] * 2,
        scratch_shapes=[pltpu.VMEM((HEADS * HD, D), bf16), pltpu.SemaphoreType.DMA],
        compiler_params=params(56),
        cost_estimate=cost(400 * 256 * HEADS * HD * FEAT * NY, 4 * 2**20),
        name="question_output",
    )(question_len, parts, w_out, after)


def total_of(*parts):
    total = parts[0].astype(f32)
    for part in parts[1:]:
        total = total + part.astype(f32)
    return total.astype(bf16)


def across_kernel(keep_ref, got_ref, first_ref, second_ref):
    first_ref[...] = total_of(keep_ref[:ROWS], got_ref[:ROWS])
    second_ref[...] = total_of(keep_ref[ROWS:], got_ref[ROWS:])


def across_sum(keep, got):
    return pl.pallas_call(
        across_kernel,
        in_specs=[vmem] * 2,
        out_specs=[vmem] * 2,
        out_shape=[jax.ShapeDtypeStruct((ROWS, FEAT), bf16)] * 2,
        compiler_params=params(),
        cost_estimate=cost(0, 0),
        name="across_sum",
    )(keep, got)


def others_kernel(near_keep, near_got, far_keep, far_got, near_a, near_b, far_a, far_b):
    near_a[...] = total_of(near_keep[:ROWS], near_got[:ROWS])
    near_b[...] = total_of(near_keep[ROWS:], near_got[ROWS:])
    far_a[...] = total_of(far_keep[:ROWS], far_got[:ROWS])
    far_b[...] = total_of(far_keep[ROWS:], far_got[ROWS:])


def others_sum(*parts):
    return pl.pallas_call(
        others_kernel,
        in_specs=[vmem] * 4,
        out_specs=[vmem] * 4,
        out_shape=[jax.ShapeDtypeStruct((ROWS, FEAT), bf16)] * 4,
        compiler_params=params(),
        cost_estimate=cost(0, 0),
        name="others_sum",
    )(*parts)


def relay_kernel(
    near_ref, far_ref, first_ref, second_ref, q_keep, q_got, _, __,
    near_out, far_out, q_own_out, q_across_out,
):
    near_out[:ROWS] = total_of(near_ref[...], first_ref[...])
    far_out[:ROWS] = total_of(far_ref[...], second_ref[...])
    for d, out in enumerate((q_own_out, near_out.at[ROWS:], q_across_out, far_out.at[ROWS:])):
        out[...] = total_of(q_keep[d], q_got[d])


def relay(*parts):
    half = jax.ShapeDtypeStruct((ROWS + QPAD, FEAT), bf16)
    return pl.pallas_call(
        relay_kernel,
        in_specs=[vmem] * 6 + [anywhere] * 2,
        out_specs=[vmem] * 4,
        out_shape=[half] * 2 + [jax.ShapeDtypeStruct((QPAD, FEAT), bf16)] * 2,
        compiler_params=params(),
        cost_estimate=cost(BLK * FEAT, BLK * FEAT * 10),
        name="relay",
    )(*parts)


def finish_kernel(
    keep, got, left_a, left_b, right_a, right_b, q_own, q_across, out_ref, question_ref
):
    out_ref[:ROWS] = total_of(keep[:ROWS], got[:ROWS], left_a[:ROWS], right_a[...])
    out_ref[ROWS:] = total_of(keep[ROWS:], got[ROWS:], left_b[...], right_b[:ROWS])
    question = total_of(q_own[...], left_a[ROWS:], right_b[ROWS:], q_across[...])
    question_ref[...] = question[:QROWS]


def finish(*parts):
    return pl.pallas_call(
        finish_kernel,
        in_specs=[vmem] * len(parts),
        out_specs=[vmem] * 2,
        out_shape=[
            jax.ShapeDtypeStruct((BLK, FEAT), bf16),
            jax.ShapeDtypeStruct((QROWS, FEAT), bf16),
        ],
        compiler_params=params(),
        cost_estimate=cost(BLK * FEAT * 4, BLK * FEAT * 10),
        name="finish",
    )(*parts)


def sum_kernel(*refs):
    total = refs[0][...].astype(f32)
    for ref in refs[1:-2]:
        total = total + ref[...].astype(f32)
    refs[-1][...] = total.astype(bf16)


def sum_of(*parts, after):
    return pl.pallas_call(
        sum_kernel,
        in_specs=[vmem] * len(parts) + [anywhere],
        out_specs=vmem,
        out_shape=jax.ShapeDtypeStruct(parts[0].shape, bf16),
        compiler_params=params(),
        cost_estimate=cost(BLK * 256 * 3, BLK * 256 * 8),
        name="sum_of",
    )(*parts, after)


def to_blocks(pairs):
    return [(a * NZ + b, c * NZ + d) for (a, b), (c, d) in pairs.items()]


def shift_y(value, by):
    pairs = [(y * NC + c, (y + by) % NY * NC + c) for y in range(NY) for c in range(NC)]
    return lax.ppermute(value, "kv", pairs)


def swap_cores(value):
    pairs = [(y * NC + c, y * NC + 1 - c) for y in range(NY) for c in range(NC)]
    return lax.ppermute(value, "kv", pairs)


def body(context, question, norm_gain, w_query, w_key, w_value, w_out, block_len, question_len):
    blk_at = lax.axis_index("blk")
    tables = [jnp.asarray(t) for t in angle_tables(np.arange(BLK))]
    tables += [jnp.asarray(t) for t in angle_tables(np.arange(N_BLK + 1) * BLK)]

    q, kv, queries = projections(
        block_len, context, question, norm_gain.reshape(1, D), w_query, w_key, w_value, tables
    )
    held = jnp.where(blk_at == 0, kv, jnp.zeros_like(kv))
    held = held + lax.ppermute(kv, "blk", to_blocks({(0, 0): (2, 0)}))
    held = held + lax.ppermute(kv, "blk", to_blocks({(0, 0): (0, 3)}))
    held = held + lax.ppermute(kv, "blk", to_blocks({(0, 0): (0, 5)}))
    queries = lax.all_to_all(queries, "blk", 0, 0)
    within = {(0, 0): (0, 1), (0, 3): (0, 4), (0, 5): (0, 6)}, {(0, 0): (0, 7), (0, 3): (0, 2)}
    second = lax.ppermute(held, "blk", to_blocks({**within[0], (2, 0): (2, 3)}))
    third = lax.ppermute(held, "blk", to_blocks({**within[1], (2, 0): (2, 5)}))
    parts, token = question_attention(block_len, queries, kv)
    held = sum_of(held, second, third, after=token)
    anchors = [held]
    for x, pairs in zip((1, 3), within):
        pairs = {(2, a): (2, b) for (_, a), (_, b) in pairs.items()}
        across = {(0, z): (x, z) for z in range(NZ)}
        anchors.append(lax.ppermute(held, "blk", to_blocks({**across, **pairs})))
    parts = lax.all_to_all(parts, "blk", 0, 0)

    products = context_attention(block_len, q, kv, anchors, w_out, token)
    keep, send = products[:NY], products[NY:]
    first, second = across_sum(keep[2], swap_cores(send[2]))
    near_a, near_b, far_a, far_b = others_sum(
        keep[1], swap_cores(send[1]), keep[3], swap_cores(send[3])
    )
    left_b, right_a = shift_y(near_b, 1), shift_y(far_a, 3)
    q_keep, q_send = question_output(question_len, parts, w_out, first)
    first, second = shift_y(first, 1), shift_y(second, 3)
    near, far, q_own, q_across = relay(
        near_a, far_b, first, second, q_keep, swap_cores(q_send), left_b, right_a
    )
    left_a, right_b = shift_y(near, 1), shift_y(far, 3)
    q_across = shift_y(q_across, 2)
    own = keep[0], swap_cores(send[0])
    return finish(*own, left_a, left_b, right_a, right_b, q_own, q_across)


def solution(mesh):
    return jax.shard_map(
        body,
        mesh=mesh,
        in_specs=(
            P("blk", None),
            P("blk", None),
            P(),
            P(None, "kv"),
            P(None, "kv"),
            P(None, "kv"),
            P("kv", None),
            P(),
            P(),
        ),
        out_specs=(P("blk", "kv"), P("blk", "kv")),
        check_vma=False,
    )
```
